128 devices in a mesh: particle: 128 (over y, z, x, core).
Axes of the slice: x: 4, y: 4, z: 4, core: 2. Of those that a mesh axis runs over, the one named last changes fastest.
Arguments:
- x_prev: bfloat16 [65536, 512], P('particle'), may hold values from -6 to 6
- anc_owner: int32 [65536, 1], P('particle'), may hold values from 0 to 127; in each aligned block of 512 rows (0 to 511, 512 to 1023, ...) at most 8 rows name the same one
- anc_row: int32 [65536], P('particle'), may hold values from 0 to 511
- noise: bfloat16 [65536, 512], P('particle'), may hold values from -6 to 6
- g_new: bfloat16 [65536, 512], P('particle'), may hold values from -6 to 6
- obs: bfloat16 [65536, 128], P('particle'), may hold values from -64 to 64
- w1: bfloat16 [512, 1024], replicated, may hold values from -0.25 to 0.25
- b1: float32 [1024], replicated, may hold values from -3 to 3
- w2: bfloat16 [1024, 512], replicated, may hold values from -0.1875 to 0.1875
- b2: float32 [512], replicated, may hold values from -3 to 3
- c_obs: bfloat16 [512, 128], replicated, may hold values from -0.25 to 0.25
- inv_scale: float32 [128], replicated, may hold values from 0.04 to 0.12
- sigma: float32 [512], replicated, may hold values from 0.1 to 0.5
Outputs:
- d_prev: float32 [65536, 512], P('particle')
- d_w1: float32 [512, 1024], replicated
- d_b1: float32 [1024], replicated
- d_w2: float32 [1024, 512], replicated
- d_b2: float32 [512], replicated
- d_c: float32 [512, 128], replicated
- d_sigma: float32 [512], replicated
The draws below stay inside these ranges and needn't reach their ends.
Inputs may be any that keep to these rules, and one draw needn't show every extreme that they name: `anc_owner`: within the 512 rows of one device no device index appears more than 8 times, and in some device's rows one appears exactly 8 times.
All inputs are finite; a program needn't handle non-finite values.
Results may differ from the reference program's by a relative error of at most 0.0056.
Values may be sent and summed in bfloat16 or wider, within the bound.
A program may use at most 64 MiB of HBM per device.

```python
import math
import jax
import jax.numpy as jnp
import numpy as np
from jax import lax

S = 512
H = 1024
OBS = 128
TOK_DEV = 512
PARTICLES = 65536
MOST = 8
N_PARTICLE = 128


def draw_obs(key, part):
    key = jax.random.fold_in(key, 11)
    key_sign, key_level, key_rough = jax.random.split(key, 3)
    signs = jnp.where(jax.random.bernoulli(key_sign, 0.5, (OBS,)), 1.0, -1.0).astype(jnp.float32)
    place = jnp.arange(PARTICLES, dtype=jnp.float32) / PARTICLES
    widen = jnp.sqrt(128.0 / OBS)
    level = jax.random.uniform(key_level, (OBS,), jnp.float32, 3.0, 6.0)
    rough = 0.5 * jax.random.truncated_normal(key_rough, -3.0, 3.0, (PARTICLES, OBS), jnp.float32)
    trend = 1.0 - 0.07 * place
    values = (widen * signs * level)[None, :] * trend[:, None] + rough
    return values.astype(jnp.bfloat16)


def place_ends(drawn, own_key, low, top_value):
    spot = [jax.random.randint(jax.random.fold_in(own_key, axis), (), 0, length) for axis, length in enumerate(drawn.shape)]
    main_axis = drawn.shape.index(max(drawn.shape))
    next_to = spot[:main_axis] + [(spot[main_axis] + 1) % drawn.shape[main_axis]] + spot[main_axis + 1:]
    return drawn.at[tuple(spot)].set(low).at[tuple(next_to)].set(top_value)


def shard_levels(key, dims, shards, least, top_value):
    level = 1.0
    for position, shards_of in shards:
        heights = jax.random.uniform(jax.random.fold_in(jax.random.fold_in(key, 6), position), (shards_of,), jnp.float32, least / len(shards), top_value / len(shards))
        level = level * jnp.repeat(jnp.exp(heights), dims[position] // shards_of).reshape((-1,) + (1,) * (len(dims) - 1 - position))
    return level


def rank_table(count, skew):
    weights = [(1 << 20) // math.isqrt(rank ** skew) + 1 for rank in range(1, count + 1)]
    scale = 1 + sum(weights) // (1 << 30)
    return np.cumsum(np.array([max(1, weight // scale) for weight in weights]))


def ranked(own_key, dims, number_of, skew):
    table = rank_table(number_of, skew)
    ticket = jax.random.randint(jax.random.fold_in(own_key, 1), dims, 0, int(table[number_of - 1]))
    grade = jnp.searchsorted(jnp.asarray(table, jnp.int32), ticket, side="right")
    return jax.random.permutation(jax.random.fold_in(own_key, 2), number_of)[grade].astype(jnp.int32)


def routed_block(stream_key, own, number, rows, number_of, top, most, skew):
    order = jax.random.permutation(stream_key, number_of)
    heavy_load, ordinary = portions_of(number_of, rows * top, most, skew, True), portions_of(number_of, rows * top, most, skew, False)
    places = jnp.arange(number_of)

    def named(lengths, rotation):
        used = int((lengths > 0).sum())
        fixed = max(1, used // 4)
        moved = fixed + (places - fixed + rotation * (used - fixed)) % max(1, number_of - fixed)
        return jnp.zeros((number_of,), jnp.int32).at[order[jnp.where(places < fixed, places, moved)]].set(jnp.asarray(lengths, jnp.int32))

    lengths = jnp.where(number % 4 == 0, named(heavy_load, number // 4), named(ordinary, number - number // 4 - 1))
    mixed = jax.random.permutation(jax.random.fold_in(own, 3), number_of)
    giver, sink = mixed[0:number_of // 2 * 2:2], mixed[1:number_of // 2 * 2:2]
    room = jnp.minimum(lengths[giver] - 1, most - lengths[sink]) // 2
    room = jnp.where((giver == order[0]) | (sink == order[0]) | (lengths[sink] == 0), 0, jnp.maximum(room, 0))
    moved = jax.random.randint(jax.random.fold_in(own, 4), (number_of // 2,), 0, 1 << 20) % (room + 1)
    lengths = lengths.at[giver].add(-moved).at[sink].add(moved)
    labels = jnp.searchsorted(jnp.cumsum(lengths), jnp.arange(rows * top), side="right").astype(jnp.int32)
    table = labels.reshape(top, rows).T
    table = table[jax.random.permutation(jax.random.fold_in(own, 1), rows)]
    rotation = jax.random.randint(jax.random.fold_in(own, 2), (rows, 1), 0, top)
    return jnp.take_along_axis(table, (jnp.arange(top)[None, :] + rotation) % top, axis=1)


def portions_of(amount, total, most, lean, full):
    portions = [(1 << 20) // math.isqrt(grade ** lean) + 1 for grade in range(1, amount + 1)]
    largest = most if full else min(most, max(-(-total // amount), total * portions[0] // sum(portions)))
    least = 1 if total - largest >= amount - 1 else 0
    holding, rest = [largest] + [least] * (amount - 1), total - largest - least * (amount - 1)
    while rest > 0:
        free = [i for i in range(1, amount) if holding[i] < largest] or [i for i in range(1, amount) if holding[i] < most]
        pool, budget = sum([portions[i] for i in free]), rest
        for i in free:
            addition = min(most - holding[i], max(1, budget * portions[i] // pool), rest)
            holding[i] = holding[i] + addition
            rest = rest - addition
    return np.array(holding)


def gaussian(own_key, dims, deviation, reach, cuts=(), held_as=jnp.bfloat16):
    factor_of = shard_levels(own_key, dims, cuts, -0.22, 0.18) if cuts else 1.0
    entries = jax.random.normal(own_key, dims, jnp.float32) * deviation * factor_of
    return jnp.minimum(jnp.maximum(entries, -reach), reach).astype(held_as)


def setup_inputs(seed: int = 0) -> dict:
    splits = jax.random.split(jax.random.key(seed), 14)
    x_prev = gaussian(splits[0], (PARTICLES, S), 1.0, 6.0, ((0, 128),))
    anc_owner_keys = jax.random.split(jax.random.fold_in(splits[1], 1), PARTICLES // TOK_DEV)
    anc_owner_turns = jax.random.permutation(jax.random.fold_in(splits[1], 3), PARTICLES // TOK_DEV)
    anc_owner = jax.vmap(lambda own, number: routed_block(jax.random.fold_in(splits[1], 2), own, number, TOK_DEV, N_PARTICLE, 1, MOST, 2))(anc_owner_keys, anc_owner_turns).reshape((PARTICLES, 1))
    anc_row = place_ends(ranked(splits[2], (PARTICLES,), TOK_DEV, 2), jax.random.fold_in(splits[2], 3), 0, TOK_DEV - 1).astype(jnp.int32)
    noise = gaussian(splits[3], (PARTICLES, S), 1.0, 6.0, ((0, 128),))
    g_new = gaussian(splits[4], (PARTICLES, S), 1.0, 6.0, ((0, 128),))
    obs = draw_obs(jax.random.fold_in(splits[13], 71), 0)
    w1 = gaussian(splits[6], (S, H), S ** -0.5, 0.25)
    b1 = gaussian(splits[7], (H,), 0.5, 3.0, (), jnp.float32)
    w2 = gaussian(splits[8], (H, S), H ** -0.5, 0.1875)
    b2 = gaussian(splits[9], (S,), 0.5, 3.0, (), jnp.float32)
    c_obs = gaussian(splits[10], (S, OBS), S ** -0.5, 0.25)
    inv_scale = jnp.clip(jnp.exp(jax.random.uniform(splits[11], (OBS,), jnp.float32, math.log(0.04), math.log(0.12))), 0.04, 0.12)
    sigma = jnp.clip(jnp.exp(jax.random.uniform(splits[12], (S,), jnp.float32, math.log(0.1), math.log(0.5))), 0.1, 0.5)
    return {"x_prev": x_prev, "anc_owner": anc_owner, "anc_row": anc_row, "noise": noise, "g_new": g_new, "obs": obs, "w1": w1, "b1": b1, "w2": w2, "b2": b2, "c_obs": c_obs, "inv_scale": inv_scale, "sigma": sigma}


HEUN = 0.25


def tdot(left, right):
    return jnp.dot(left.astype(jnp.float32).T, right.astype(jnp.float32), precision=lax.Precision.HIGHEST)


def rdot(left, right):
    return jnp.dot(left.astype(jnp.float32), right.astype(jnp.float32).T, precision=lax.Precision.HIGHEST)


def forward(x_start, noise, obs, w1, b1, w2, b2, c_obs, inv_scale, sigma):
    t_zero = jnp.tanh(jnp.dot(x_start, w1, preferred_element_type=jnp.float32) + b1)
    a_zero = t_zero.astype(jnp.bfloat16)
    f_zero = jnp.dot(a_zero, w2, preferred_element_type=jnp.float32) + b2
    kick = sigma * noise.astype(jnp.float32)
    x_pred = (x_start.astype(jnp.float32) + HEUN * f_zero + kick).astype(jnp.bfloat16)
    t_one = jnp.tanh(jnp.dot(x_pred, w1, preferred_element_type=jnp.float32) + b1)
    a_one = t_one.astype(jnp.bfloat16)
    f_one = jnp.dot(a_one, w2, preferred_element_type=jnp.float32) + b2
    x_next = x_start.astype(jnp.float32) + 0.5 * HEUN * (f_zero + f_one) + kick
    x_round = x_next.astype(jnp.bfloat16)
    resid = (obs.astype(jnp.float32) - jnp.dot(x_round, c_obs, preferred_element_type=jnp.float32)) * inv_scale
    loglik = -0.5 * jnp.sum(resid * resid, axis=1)
    return loglik, (t_zero, a_zero, x_pred, t_one, a_one, x_round, resid)


def backward(x_start, noise, g_new, weight_q, saved, w1, w2, c_obs, inv_scale):
    t_zero, a_zero, x_pred, t_one, a_one, x_round, resid = saved
    dmean = (weight_q[:, None] * resid * inv_scale).astype(jnp.bfloat16)
    gxn = g_new.astype(jnp.float32) + rdot(dmean, c_obs)
    d_c = tdot(x_round, dmean)
    gf_one = 0.5 * HEUN * gxn
    gf_one_b = gf_one.astype(jnp.bfloat16)
    gp_one = rdot(gf_one_b, w2) * (1.0 - t_one * t_one)
    gp_one_b = gp_one.astype(jnp.bfloat16)
    gxp = rdot(gp_one_b, w1)
    gf_zero = 0.5 * HEUN * gxn + HEUN * gxp
    gf_zero_b = gf_zero.astype(jnp.bfloat16)
    gp_zero = rdot(gf_zero_b, w2) * (1.0 - t_zero * t_zero)
    gp_zero_b = gp_zero.astype(jnp.bfloat16)
    gx_zero = gxn + gxp + rdot(gp_zero_b, w1)
    d_w2 = tdot(a_one, gf_one_b) + tdot(a_zero, gf_zero_b)
    d_b2 = jnp.sum(gf_one + gf_zero, axis=0)
    d_w1 = tdot(x_pred, gp_one_b) + tdot(x_start, gp_zero_b)
    d_b1 = jnp.sum(gp_one + gp_zero, axis=0)
    d_sigma = jnp.sum((gxn + gxp) * noise.astype(jnp.float32), axis=0)
    return gx_zero, (d_w1, d_b1, d_w2, d_b2, d_c, d_sigma)


def reference(x_prev, anc_owner, anc_row, noise, g_new, obs, w1, b1, w2, b2, c_obs, inv_scale, sigma):
    ancestor = (anc_owner[:, 0] * TOK_DEV + anc_row).astype(jnp.int32)
    x_start = x_prev[ancestor]
    blocks = N_PARTICLE
    xs = x_start.reshape(blocks, TOK_DEV, S)
    ns = noise.reshape(blocks, TOK_DEV, S)
    gs = g_new.reshape(blocks, TOK_DEV, S)
    os_ = obs.reshape(blocks, TOK_DEV, OBS)

    def first(item):
        return forward(item[0], item[1], item[2], w1, b1, w2, b2, c_obs, inv_scale, sigma)[0]

    loglik = lax.map(first, (xs, ns, os_))
    peak = jnp.max(loglik)
    total = jnp.sum(jnp.exp(loglik - peak))
    weight_q = jnp.exp(loglik - peak) / total * PARTICLES

    def second(carry, item):
        x_blk, n_blk, g_blk, o_blk, q_blk = item
        _, saved = forward(x_blk, n_blk, o_blk, w1, b1, w2, b2, c_obs, inv_scale, sigma)
        gx_zero, grads = backward(x_blk, n_blk, g_blk, q_blk, saved, w1, w2, c_obs, inv_scale)
        return tuple(c + g for c, g in zip(carry, grads)), gx_zero

    init = (jnp.zeros((S, H), jnp.float32), jnp.zeros((H,), jnp.float32), jnp.zeros((H, S), jnp.float32),
            jnp.zeros((S,), jnp.float32), jnp.zeros((S, OBS), jnp.float32), jnp.zeros((S,), jnp.float32))
    grads, gx_all = lax.scan(second, init, (xs, ns, gs, os_, weight_q))
    d_prev = jnp.zeros((PARTICLES, S), jnp.float32).at[ancestor].add(gx_all.reshape(PARTICLES, S))
    return d_prev, grads[0], grads[1], grads[2], grads[3], grads[4], grads[5]
```

```python
import functools

import jax
import jax.numpy as jnp
from jax import lax
from jax.experimental import pallas as pl
from jax.experimental.pallas import tpu as pltpu
from jax.sharding import PartitionSpec as P

MESH = pl.DeviceIdType.MESH
HEUN = 0.25
F32 = jnp.float32
BF16 = jnp.bfloat16
I32 = jnp.int32
MOST = 8
LOGSTEP = 65536.0
TOP = 32767.0


def nn(left, right):
    return jnp.dot(left, right, preferred_element_type=F32)


def nt(left, right):
    return lax.dot_general(left, right, (((1,), (1,)), ((), ())), preferred_element_type=F32)


def tn(left, right):
    return lax.dot_general(left, right, (((0,), (0,)), ((), ())), preferred_element_type=F32)


def iota(shape, dim):
    return lax.broadcasted_iota(I32, shape, dim)


def split(value):
    high = value.astype(BF16)
    return high, (value - high.astype(F32)).astype(BF16)


def encode(value):
    peak = jnp.max(jnp.max(jnp.abs(value), axis=2, keepdims=True), axis=1, keepdims=True)
    level = jnp.ceil(jnp.log(jnp.maximum(peak, 1e-30)) * LOGSTEP).astype(I32)
    scale = TOP * jnp.exp(level.astype(F32) * (-1.0 / LOGSTEP))
    code = jnp.round(value * scale).astype(I32)
    return code, jnp.broadcast_to(level, (value.shape[0], 1, 128))


def pack(low, high):
    return jnp.bitwise_or(jnp.left_shift(high, 16), jnp.bitwise_and(low, 0xFFFF))


def unpack(word):
    low = jnp.right_shift(jnp.left_shift(word, 16), 16)
    return low.astype(F32), jnp.right_shift(word, 16).astype(F32)


def encode_wide(value):
    code, level = encode(value)
    word = pack(code[:, :, :256], code[:, :, 256:])
    return jnp.concatenate([word[:, :, :128], word[:, :, 128:]], axis=1), level


def unscale(level):
    return jnp.exp(level.astype(F32) * (1.0 / LOGSTEP)) * (1.0 / TOP)


def decode_wide(word, level):
    scale = unscale(level)
    low0, high0 = unpack(word[:, :8])
    low1, high1 = unpack(word[:, 8:])
    return jnp.concatenate([low0 * scale, low1 * scale, high0 * scale, high1 * scale], axis=2)


def encode_slice(one, two, rest):
    word1, level1 = encode_wide(one)
    word2, level2 = encode_wide(two)
    code3, level3 = encode(rest)
    word3 = pack(code3[:, :4], code3[:, 4:])
    return jnp.concatenate([word1, word2, word3, level1, level2, level3, level3], axis=1)


def decode_slice(word):
    one = decode_wide(word[:, 0:16], word[:, 36:37])
    two = decode_wide(word[:, 16:32], word[:, 37:38])
    scale = unscale(word[:, 38:39])
    low, high = unpack(word[:, 32:36])
    return one, two, jnp.concatenate([low * scale, high * scale], axis=1)


def wanted_columns(table):
    shape = (1, MOST, 128)
    lane, sub = iota(shape, 2), iota(shape, 1)
    one = jnp.where((lane == sub) | (lane == sub + 2 * MOST), 1.0, 0.0)
    weight = jnp.where(lane == sub + MOST, 256.0, one)
    return jnp.sum(table * weight, axis=2, keepdims=True) - 1.0


def bytes_wait(ref, semaphore):
    pltpu.make_async_copy(ref, ref, semaphore).wait()


def main_kernel(
    devices,
    x_ref, owner_ref, row_ref, noise_ref, g_ref, obs_ref, w1_ref, b1_ref, w2_ref, b2_ref, c_ref, inv_ref, sigma_ref,
    inc_ref, arr_ref, all_ref,
    wtab, wrow, send_rows, recv_rows, norm_src, norm_tab, ret, xx, aa, gf, gp, u0, u1, xnb, f0s, gxs, dots,
    acc1, acc2, accx, in1, in2, inx, enc, got, fin,
    ssem, rsem,
):
    me = lax.axis_index("particle")
    rows, width = x_ref.shape
    hidden = w1_ref.shape[1]
    chips = devices // 2
    chip, core = lax.div(me, 2), lax.rem(me, 2)
    other = me + 1 - 2 * core

    barrier = pltpu.get_barrier_semaphore()

    def greet(k, carry):
        pl.semaphore_signal(barrier, inc=1, device_id=(lax.rem(me + k, devices),), device_id_type=MESH)
        return carry

    lax.fori_loop(1, devices, greet, 0)

    owner = owner_ref[...]
    row = row_ref[...]
    named = jnp.where(iota((devices, rows), 0) == owner, 1.0, 0.0)
    named_b = named.astype(BF16)
    earlier = jnp.where(iota((rows, rows), 0) < iota((rows, rows), 1), 1.0, 0.0).astype(BF16)
    slot = jnp.sum(nn(named_b, earlier) * named, axis=0, keepdims=True)
    part = iota((128, rows), 0)
    low = jnp.bitwise_and(row, 255).astype(F32)
    high = jnp.right_shift(row, 8).astype(F32)
    value = jnp.where(part < MOST, low, jnp.where(part < 2 * MOST, high, jnp.where(part < 3 * MOST, 1.0, 0.0)))
    value = jnp.where(jnp.bitwise_and(part, MOST - 1).astype(F32) == slot, value, 0.0)
    wrow[...] = nt(named_b, value.astype(BF16))

    def spread(d, carry):
        wtab[d] = wrow[pl.ds(d, 1), :]
        return carry

    lax.fori_loop(0, devices, spread, 0, unroll=8)
    eye = jnp.where(iota((rows, rows), 0) == iota((rows, rows), 1), 1.0, 0.0).astype(BF16)
    pair = jnp.where(part == 0, owner.astype(F32), jnp.where(part == 1, slot, 0.0)).astype(BF16)
    turned = nt(eye, pair)
    place = turned[:, 0:1] * (2 * MOST) + turned[:, 1:2]
    flat = owner * MOST + slot.astype(I32)

    pl.semaphore_wait(barrier, devices - 1)

    def exchange(stage, source, target, partner_block):
        def send(k, carry):
            d = lax.rem(me + k, devices)
            pltpu.make_async_remote_copy(
                src_ref=source.at[d] if partner_block else source.at[0],
                dst_ref=target.at[me],
                send_sem=ssem.at[stage],
                recv_sem=rsem.at[stage],
                device_id=(d,),
                device_id_type=MESH,
            ).start()
            return carry

        lax.fori_loop(1, devices, send, 0)

    def exchange_wait(stage, target):
        most = target.at[pl.ds(0, devices - 1)]
        bytes_wait(most, ssem.at[stage])
        bytes_wait(most, rsem.at[stage])

    exchange(0, wtab, inc_ref, True)
    inc_ref[me] = wtab[me]
    exchange_wait(0, inc_ref)

    group = 16

    def gather(i, carry):
        at = pl.multiple_of(i * group, group)
        column = wanted_columns(inc_ref[pl.ds(at, group)])
        onehot = jnp.where(column == iota((group, MOST, rows), 2).astype(F32), 1.0, 0.0)
        out = nn(onehot.reshape(group * MOST, rows).astype(BF16), x_ref[...])
        halves = jnp.concatenate(
            [out[:, : width // 2].reshape(group, MOST, width // 2), out[:, width // 2 :].reshape(group, MOST, width // 2)],
            axis=1,
        )
        send_rows[pl.ds(at, group)] = halves.astype(BF16)
        return carry

    lax.fori_loop(0, devices // group, gather, 0)
    exchange(1, send_rows, recv_rows, True)
    recv_rows[me] = send_rows[me]
    exchange_wait(1, recv_rows)

    def start(i, carry):
        left, right = carry
        at = pl.multiple_of(i * group, group)
        block = recv_rows[pl.ds(at, group)].reshape(group * 2 * MOST, width // 2)
        index = (iota((rows, group * 2 * MOST), 1) + at * (2 * MOST)).astype(F32)
        take_left = jnp.where(place == index, 1.0, 0.0).astype(BF16)
        take_right = jnp.where(place + MOST == index, 1.0, 0.0).astype(BF16)
        return left + nn(take_left, block), right + nn(take_right, block)

    none = jnp.zeros((rows, width // 2), F32)
    left, right = lax.fori_loop(0, devices // group, start, (none, none))
    xx[rows:, : width // 2] = left.astype(BF16)
    xx[rows:, width // 2 :] = right.astype(BF16)

    x0 = xx[rows:, :]
    block = 256
    for n in range(0, hidden, block):
        t = jnp.tanh(nn(x0, w1_ref[:, n : n + block]) + b1_ref[:, n : n + block])
        aa[rows:, n : n + block] = t.astype(BF16)
        u0[:, n : n + block] = 1.0 - t * t
    for n in range(0, width, block):
        cols = slice(n, n + block)
        f = nn(aa[rows:, :], w2_ref[:, cols]) + b2_ref[:, cols]
        kick = sigma_ref[:, cols] * noise_ref[:, cols].astype(F32)
        f0s[:, cols] = f
        xx[:rows, cols] = (xx[rows:, cols].astype(F32) + HEUN * f + kick).astype(BF16)
    xp = xx[:rows, :]
    for n in range(0, hidden, block):
        t = jnp.tanh(nn(xp, w1_ref[:, n : n + block]) + b1_ref[:, n : n + block])
        aa[:rows, n : n + block] = t.astype(BF16)
        u1[:, n : n + block] = 1.0 - t * t
    for n in range(0, width, block):
        cols = slice(n, n + block)
        f = nn(aa[:rows, :], w2_ref[:, cols]) + b2_ref[:, cols]
        kick = sigma_ref[:, cols] * noise_ref[:, cols].astype(F32)
        xn = xx[rows:, cols].astype(F32) + 0.5 * HEUN * (f0s[:, cols] + f) + kick
        xnb[:, cols] = xn.astype(BF16)
    resid = (obs_ref[...].astype(F32) - nn(xnb[...], c_ref[...])) * inv_ref[...]
    loglik = -0.5 * jnp.sum(resid * resid, axis=1, keepdims=True)

    peak = jnp.max(loglik, axis=0, keepdims=True)
    total = jnp.sum(jnp.exp(loglik - peak), axis=0, keepdims=True)
    norm_src[0] = jnp.where(iota((1, 128), 1) == 0, peak, total)
    exchange(2, norm_src, norm_tab, False)
    norm_tab[me] = norm_src[0]
    exchange_wait(2, norm_tab)
    table = norm_tab[...]
    peaks, totals = table[:, :, 0:1], table[:, :, 1:2]
    top = jnp.max(peaks, axis=0, keepdims=True)
    whole = jnp.sum(totals * jnp.exp(peaks - top), axis=0, keepdims=True)
    weight = jnp.exp(loglik - top[0]) / whole[0] * float(rows * devices)

    dmean = (weight * resid * inv_ref[...]).astype(BF16)
    for n in range(0, width, block):
        cols = slice(n, n + block)
        gxn = g_ref[:, cols].astype(F32) + nt(dmean, c_ref[cols, :])
        gxs[:, cols] = gxn
        gf[:rows, cols] = (0.5 * HEUN * gxn).astype(BF16)
    for n in range(0, hidden, block):
        cols = slice(n, n + block)
        one = nt(gf[:rows, :], w2_ref[cols, :]) * u1[:, cols]
        gp[:rows, cols] = one.astype(BF16)
        dots[:, cols] = jnp.sum(one, axis=0, keepdims=True)
    for n in range(0, width, block):
        cols = slice(n, n + block)
        gxn = gxs[:, cols]
        gxp = nt(gp[:rows, :], w1_ref[cols, :])
        both = gxn + gxp
        gf0 = 0.5 * HEUN * gxn + HEUN * gxp
        gf[rows:, cols] = gf0.astype(BF16)
        gxs[:, cols] = both
        d_b2 = jnp.sum(0.5 * HEUN * gxn + gf0, axis=0, keepdims=True)
        d_sigma = jnp.sum(both * noise_ref[:, cols].astype(F32), axis=0, keepdims=True)
        for j in range(block // 128):
            at = n // 128 + j
            accx[1, 1, at : at + 1, :] = d_b2[:, 128 * j : 128 * (j + 1)]
            accx[1, 2, at : at + 1, :] = d_sigma[:, 128 * j : 128 * (j + 1)]
    for n in range(0, hidden, block):
        cols = slice(n, n + block)
        zero = nt(gf[rows:, :], w2_ref[cols, :]) * u0[:, cols]
        gp[rows:, cols] = zero.astype(BF16)
        d_b1 = dots[:, cols] + jnp.sum(zero, axis=0, keepdims=True)
        for j in range(block // 128):
            at = n // 128 + j
            accx[1, 0, at : at + 1, :] = d_b1[:, 128 * j : 128 * (j + 1)]
    for n in range(0, width, block):
        cols = slice(n, n + block)
        gxs[:, cols] = gxs[:, cols] + nt(gp[rows:, :], w1_ref[cols, :])

    gx_high, gx_low = split(gxs[...])

    def give(i, carry):
        at = pl.multiple_of(i * group, group)
        onehot = jnp.where(iota((group * MOST, rows), 0) + at * MOST == flat, 1.0, 0.0).astype(BF16)
        out = nn(onehot, gx_high) + nn(onehot, gx_low)
        word, level = encode_wide(out.reshape(group, MOST, width))
        ret[pl.ds(at, group)] = jnp.concatenate([word, level], axis=1)
        return carry

    lax.fori_loop(0, devices // group, give, 0)
    exchange(3, ret, arr_ref, True)
    arr_ref[me] = ret[me]

    accx[1, 1, 4:8, :] = jnp.zeros((4, 128), F32)
    accx[1, 2, 4:8, :] = jnp.zeros((4, 128), F32)
    accx[1, pl.ds(3, chips - 3)] = jnp.zeros((chips - 3, 8, 128), F32)
    accx[0] = tn(xnb[...], dmean).reshape(chips, 8, 128)
    for n in range(0, hidden, block):
        acc2[n // 8 : (n + block) // 8] = tn(aa[:, n : n + block], gf[...]).reshape(block // 8, 8, width)
    for h in range(2):
        acc1[h * chips : (h + 1) * chips] = tn(xx[...], gp[:, h * width : (h + 1) * width]).reshape(chips, 8, width)

    swaps = []
    for i, (source, target) in enumerate(
        (
            (acc1.at[pl.ds((1 - core) * chips, chips)], in1),
            (acc2.at[pl.ds((1 - core) * chips, chips)], in2),
            (accx.at[1 - core], inx),
        )
    ):
        swap = pltpu.make_async_remote_copy(
            src_ref=source, dst_ref=target, send_sem=ssem.at[4 + i], recv_sem=rsem.at[4 + i],
            device_id=(other,), device_id_type=MESH,
        )
        swap.start()
        swaps.append(swap)
    for swap in swaps:
        swap.wait()

    step = 4

    def prepare(i, carry):
        at = pl.multiple_of(i * step, step)
        mine = pl.ds(at, step)
        held = pl.ds(core * chips + at, step)
        in1[mine] = in1[mine] + acc1[held]
        in2[mine] = in2[mine] + acc2[held]
        inx[mine] = inx[mine] + accx[core, mine]
        enc[mine] = encode_slice(in1[mine], in2[mine], inx[mine])
        return carry

    lax.fori_loop(0, chips // step, prepare, 0)

    def chips_send(stage, source, target):
        def send(k, carry):
            c = lax.rem(chip + k, chips)
            pltpu.make_async_remote_copy(
                src_ref=source(c), dst_ref=target, send_sem=ssem.at[stage], recv_sem=rsem.at[stage],
                device_id=(2 * c + core,), device_id_type=MESH,
            ).start()
            return carry

        lax.fori_loop(1, chips, send, 0)

    def chips_wait(stage, target):
        bytes_wait(target, ssem.at[stage])
        bytes_wait(target, rsem.at[stage])

    chips_send(7, lambda c: enc.at[c], got.at[chip])
    got[chip] = enc[chip]
    chips_wait(7, got.at[pl.ds(0, chips - 1)])

    def add(i, carry):
        one, two, rest = decode_slice(got[pl.ds(i, 1)])
        return carry[0] + one, carry[1] + two, carry[2] + rest

    zeros = (jnp.zeros((1, 8, width), F32), jnp.zeros((1, 8, width), F32), jnp.zeros((1, 8, 128), F32))
    sums = lax.fori_loop(0, chips, add, zeros)
    fin[...] = encode_slice(*sums)

    chips_send(8, lambda c: fin.at[0], all_ref.at[core, chip])
    all_ref[core, chip] = fin[0]
    chips_wait(8, all_ref.at[0, pl.ds(0, chips - 1)])

    last = pltpu.make_async_remote_copy(
        src_ref=all_ref.at[core], dst_ref=all_ref.at[core], send_sem=ssem.at[9], recv_sem=rsem.at[9],
        device_id=(other,), device_id_type=MESH,
    )
    last.start()
    last.wait()
    exchange_wait(3, arr_ref)


def finish_kernel(inc_ref, arr_ref, all_ref, dprev_ref, dw1_ref, dw2_ref, dc_ref, db1_ref, db2_ref, dsigma_ref):
    devices = inc_ref.shape[0]
    chips = devices // 2
    rows, width = dprev_ref.shape
    group = 16

    def place(i, carry):
        at = pl.multiple_of(i * group, group)
        column = wanted_columns(inc_ref[pl.ds(at, group)])
        onehot = jnp.where(column == iota((group, MOST, rows), 2).astype(F32), 1.0, 0.0)
        onehot = onehot.reshape(group * MOST, rows).astype(BF16)
        word = arr_ref[pl.ds(at, group)]
        value = decode_wide(word[:, :16], word[:, 16:17]).reshape(group * MOST, width)
        high, low = split(value)
        return carry + tn(onehot, high) + tn(onehot, low)

    dprev_ref[...] = lax.fori_loop(0, devices // group, place, jnp.zeros((rows, width), F32))

    step = 4
    for core in range(2):

        def spread(i, carry):
            at = pl.multiple_of(i * step, step)
            one, two, rest = decode_slice(all_ref[core, pl.ds(at, step)])
            lines = pl.ds(pl.multiple_of(at * 8, step * 8), step * 8)
            dw1_ref[lines, core * width : (core + 1) * width] = one.reshape(step * 8, width)
            far = pl.ds(pl.multiple_of(at * 8 + core * chips * 8, step * 8), step * 8)
            dw2_ref[far, :] = two.reshape(step * 8, width)
            if core == 0:
                dc_ref[lines, :] = rest.reshape(step * 8, 128)
            return carry

        lax.fori_loop(0, chips // step, spread, 0)
    _, _, small = decode_slice(all_ref[1, 0:3])
    db1_ref[...] = small[0]
    db2_ref[...] = small[1, :4]
    dsigma_ref[...] = small[2, :4]


def per_device(x_prev, anc_owner, anc_row, noise, g_new, obs, w1, b1, w2, b2, c_obs, inv_scale, sigma):
    devices = lax.axis_size("particle")
    chips = devices // 2
    rows, width = x_prev.shape
    hidden = w1.shape[1]
    vmem = pl.BlockSpec(memory_space=pltpu.VMEM)
    inc, arr, whole = pl.pallas_call(
        functools.partial(main_kernel, devices),
        out_shape=(
            jax.ShapeDtypeStruct((devices, 1, 128), F32),
            jax.ShapeDtypeStruct((devices, 17, 128), I32),
            jax.ShapeDtypeStruct((2, chips, 40, 128), I32),
        ),
        in_specs=[vmem] * 13,
        out_specs=(vmem, vmem, vmem),
        scratch_shapes=[
            pltpu.VMEM((devices, 1, 128), F32),
            pltpu.VMEM((devices, 128), F32),
            pltpu.VMEM((devices, 2 * MOST, width // 2), BF16),
            pltpu.VMEM((devices, 2 * MOST, width // 2), BF16),
            pltpu.VMEM((1, 1, 128), F32),
            pltpu.VMEM((devices, 1, 128), F32),
            pltpu.VMEM((devices, 17, 128), I32),
            pltpu.VMEM((2 * rows, width), BF16),
            pltpu.VMEM((2 * rows, hidden), BF16),
            pltpu.VMEM((2 * rows, width), BF16),
            pltpu.VMEM((2 * rows, hidden), BF16),
            pltpu.VMEM((rows, hidden), F32),
            pltpu.VMEM((rows, hidden), F32),
            pltpu.VMEM((rows, width), BF16),
            pltpu.VMEM((rows, width), F32),
            pltpu.VMEM((rows, width), F32),
            pltpu.VMEM((1, hidden), F32),
            pltpu.VMEM((devices, 8, width), F32),
            pltpu.VMEM((devices, 8, width), F32),
            pltpu.VMEM((2, chips, 8, 128), F32),
            pltpu.VMEM((chips, 8, width), F32),
            pltpu.VMEM((chips, 8, width), F32),
            pltpu.VMEM((chips, 8, 128), F32),
            pltpu.VMEM((chips, 40, 128), I32),
            pltpu.VMEM((chips, 40, 128), I32),
            pltpu.VMEM((1, 40, 128), I32),
            pltpu.SemaphoreType.DMA((10,)),
            pltpu.SemaphoreType.DMA((10,)),
        ],
        compiler_params=pltpu.CompilerParams(collective_id=0, has_side_effects=True, vmem_limit_bytes=56 * 2**20),
        name="heun_step",
    )(
        x_prev, anc_owner.reshape(1, rows), anc_row.reshape(1, rows), noise, g_new, obs,
        w1, b1.reshape(1, hidden), w2, b2.reshape(1, width), c_obs, inv_scale.reshape(1, -1), sigma.reshape(1, width),
    )
    d_prev, d_w1, d_w2, d_c, d_b1, d_b2, d_sigma = pl.pallas_call(
        finish_kernel,
        out_shape=(
            jax.ShapeDtypeStruct((rows, width), F32),
            jax.ShapeDtypeStruct((width, hidden), F32),
            jax.ShapeDtypeStruct((hidden, width), F32),
            jax.ShapeDtypeStruct((width, 128), F32),
            jax.ShapeDtypeStruct((hidden // 128, 128), F32),
            jax.ShapeDtypeStruct((width // 128, 128), F32),
            jax.ShapeDtypeStruct((width // 128, 128), F32),
        ),
        in_specs=[vmem] * 3,
        out_specs=(vmem,) * 7,
        compiler_params=pltpu.CompilerParams(vmem_limit_bytes=40 * 2**20),
        name="place_results",
    )(inc, arr, whole)
    return (d_prev, d_w1, d_b1.reshape(hidden), d_w2, d_b2.reshape(width), d_c, d_sigma.reshape(width))


def solution(mesh):
    split_rows = P("particle", None)
    return jax.shard_map(
        per_device,
        mesh=mesh,
        in_specs=(split_rows, split_rows, P("particle"), split_rows, split_rows, split_rows) + (P(),) * 7,
        out_specs=(split_rows, P(), P(), P(), P(), P(), P()),
        check_vma=False,
    )
```

```python
import functools

import jax
import jax.numpy as jnp
from jax import lax
from jax.experimental import pallas as pl
from jax.experimental.pallas import tpu as pltpu
from jax.sharding import PartitionSpec as P

MESH = pl.DeviceIdType.MESH
HEUN = 0.25
F32 = jnp.float32
BF16 = jnp.bfloat16
I32 = jnp.int32
HOP, BACK = 11, 35
MOST = 8
LOGSTEP = 65536.0
TOP = 32767.0


def nn(left, right):
    return jnp.dot(left, right, preferred_element_type=F32)


def nt(left, right):
    return lax.dot_general(left, right, (((1,), (1,)), ((), ())), preferred_element_type=F32)


def tn(left, right):
    return lax.dot_general(left, right, (((0,), (0,)), ((), ())), preferred_element_type=F32)


def iota(shape, dim):
    return lax.broadcasted_iota(I32, shape, dim)


def split(value):
    high = value.astype(BF16)
    return high, (value - high.astype(F32)).astype(BF16)


def encode(value):
    peak = jnp.max(jnp.max(jnp.abs(value), axis=2, keepdims=True), axis=1, keepdims=True)
    level = jnp.ceil(jnp.log(jnp.maximum(peak, 1e-30)) * LOGSTEP).astype(I32)
    scale = TOP * jnp.exp(level.astype(F32) * (-1.0 / LOGSTEP))
    code = jnp.round(value * scale).astype(I32)
    return code, jnp.broadcast_to(level, (value.shape[0], 1, 128))


def pack(low, high):
    return jnp.bitwise_or(jnp.left_shift(high, 16), jnp.bitwise_and(low, 0xFFFF))


def unpack(word):
    low = jnp.right_shift(jnp.left_shift(word, 16), 16)
    return low.astype(F32), jnp.right_shift(word, 16).astype(F32)


def encode_wide(value):
    code, level = encode(value)
    word = pack(code[:, :, :256], code[:, :, 256:])
    return jnp.concatenate([word[:, :, :128], word[:, :, 128:]], axis=1), level


def unscale(level):
    return jnp.exp(level.astype(F32) * (1.0 / LOGSTEP)) * (1.0 / TOP)


def decode_wide(word, level):
    scale = unscale(level)
    low0, high0 = unpack(word[:, :8])
    low1, high1 = unpack(word[:, 8:])
    return jnp.concatenate([low0 * scale, low1 * scale, high0 * scale, high1 * scale], axis=2)


def encode_slice(value):
    codes, levels = zip(*(encode(value[:, :, 128 * b : 128 * (b + 1)]) for b in range(3)))
    lane = iota((value.shape[0], 1, 128), 2)
    level = jnp.where(lane == 0, levels[0], jnp.where(lane == 1, levels[1], levels[2]))
    return jnp.concatenate([pack(codes[0], codes[1]), pack(codes[2][:, :4], codes[2][:, 4:]), level], axis=1)


def decode_slice(word):
    scale = unscale(word[:, 12:13])
    low, high = unpack(word[:, :8])
    top, bottom = unpack(word[:, 8:12])
    last = jnp.concatenate([top, bottom], axis=1)
    return low * scale[:, :, 0:1], high * scale[:, :, 1:2], last * scale[:, :, 2:3]


def joined(blocks):
    return jnp.concatenate(blocks, axis=2)


def wanted_columns(table):
    shape = (1, MOST, 128)
    lane, sub = iota(shape, 2), iota(shape, 1)
    one = jnp.where((lane == sub) | (lane == sub + 2 * MOST), 1.0, 0.0)
    weight = jnp.where(lane == sub + MOST, 256.0, one)
    return jnp.sum(table * weight, axis=2, keepdims=True) - 1.0


def bytes_wait(ref, semaphore):
    pltpu.make_async_copy(ref, ref, semaphore).wait()


def main_kernel(
    devices,
    x_hbm, owner_ref, row_ref, noise_hbm, g_hbm, obs_hbm, w1_hbm, b1_ref, w2_hbm, b2_ref, c_hbm, inv_ref, sigma_ref,
    dprev_hbm, all_hbm,
    x_ref, noise_ref, g_ref, obs_ref, w1_ref, w2_ref, c_ref, dprev, inc_ref, arr_ref,
    wtab, wrow, send_rows, recv_rows, norm_src, norm_tab, ret, xx, aa, gf, gp, u0, u1, xnb, f0s, gxs, dots,
    acc1, acc2, accx, in1, in2, inx, sums, enc1, got1, half, enc2, got2, fin, whole,
    ssem, rsem, lsem, s1, r1, s2, r2, s3, r3, s4, r4, s5, r5, out_sem,
):
    me = lax.axis_index("particle")
    rows, width = x_ref.shape
    hidden = w1_ref.shape[1]
    chips = devices // 2
    core = lax.rem(me, 2)
    other = me + 1 - 2 * core
    stride = {"x": 2, "z": 8, "y": 32}
    coordinate = {axis: lax.rem(lax.div(me, by), 4) for axis, by in stride.items()}
    streams = (("x", "y", "z"), ("z", "x", "y"), ("y", "z", "x"))

    barrier = pltpu.get_barrier_semaphore()

    def greet(k, carry):
        pl.semaphore_signal(barrier, inc=1, device_id=(lax.rem(me + k, devices),), device_id_type=MESH)
        return carry

    lax.fori_loop(1, devices, greet, 0)
    loads = [
        pltpu.make_async_copy(source, target, lsem.at[i])
        for i, (source, target) in enumerate(
            (
                (x_hbm, x_ref),
                (w1_hbm, w1_ref),
                (w2_hbm, w2_ref),
                (noise_hbm, noise_ref),
                (g_hbm, g_ref),
                (obs_hbm, obs_ref),
                (c_hbm, c_ref),
            )
        )
    ]
    for load in loads:
        load.start()

    owner = owner_ref[...]
    row = row_ref[...]
    named = jnp.where(iota((devices, rows), 0) == owner, 1.0, 0.0)
    named_b = named.astype(BF16)
    earlier = jnp.where(iota((rows, rows), 0) < iota((rows, rows), 1), 1.0, 0.0).astype(BF16)
    slot = jnp.sum(nn(named_b, earlier) * named, axis=0, keepdims=True)
    part = iota((128, rows), 0)
    low = jnp.bitwise_and(row, 255).astype(F32)
    high = jnp.right_shift(row, 8).astype(F32)
    value = jnp.where(part < MOST, low, jnp.where(part < 2 * MOST, high, jnp.where(part < 3 * MOST, 1.0, 0.0)))
    value = jnp.where(jnp.bitwise_and(part, MOST - 1).astype(F32) == slot, value, 0.0)
    wrow[...] = nt(named_b, value.astype(BF16))

    def spread(d, carry):
        wtab[d] = wrow[pl.ds(d, 1), :]
        return carry

    lax.fori_loop(0, devices, spread, 0, unroll=8)
    eye = jnp.where(iota((rows, rows), 0) == iota((rows, rows), 1), 1.0, 0.0).astype(BF16)
    turn = jnp.bitwise_and((me - owner + devices) * BACK, devices - 1)
    pair = jnp.where(part == 0, turn.astype(F32), jnp.where(part == 1, slot, 0.0)).astype(BF16)
    turned = nt(eye, pair)
    place = turned[:, 0:1] * (2 * MOST) + turned[:, 1:2]
    flat = owner * MOST + slot.astype(I32)

    pl.semaphore_wait(barrier, devices - 1)

    def exchange(stage, source, target, per_partner, by_turn=False):
        def send(k, carry):
            d = lax.rem(me + lax.rem(HOP * k, devices), devices)
            pltpu.make_async_remote_copy(
                src_ref=source.at[d] if per_partner else source.at[0],
                dst_ref=target.at[k] if by_turn else target.at[me],
                send_sem=ssem.at[stage],
                recv_sem=rsem.at[4 + lax.div(k, devices // 4)] if by_turn else rsem.at[stage],
                device_id=(d,),
                device_id_type=MESH,
            ).start()
            return carry

        lax.fori_loop(1, devices, send, 0)

    def exchange_wait(stage, target):
        most = target.at[pl.ds(0, devices - 1)]
        bytes_wait(most, ssem.at[stage])
        bytes_wait(most, rsem.at[stage])

    exchange(0, wtab, inc_ref, True)
    inc_ref[me] = wtab[me]
    exchange_wait(0, inc_ref)

    group = 16

    def gather(i, carry):
        at = pl.multiple_of(i * group, group)
        column = wanted_columns(inc_ref[pl.ds(at, group)])
        onehot = jnp.where(column == iota((group, MOST, rows), 2).astype(F32), 1.0, 0.0)
        out = nn(onehot.reshape(group * MOST, rows).astype(BF16), x_ref[...])
        halves = jnp.concatenate(
            [out[:, : width // 2].reshape(group, MOST, width // 2), out[:, width // 2 :].reshape(group, MOST, width // 2)],
            axis=1,
        )
        send_rows[pl.ds(at, group)] = halves.astype(BF16)
        return carry

    loads[0].wait()
    lax.fori_loop(0, devices // group, gather, 0)
    exchange(1, send_rows, recv_rows, True, by_turn=True)
    recv_rows[0] = send_rows[me]
    for load in loads[1:]:
        load.wait()

    left = jnp.zeros((rows, width // 2), F32)
    right = left
    quarter = devices // 4
    for i in range(4):
        first = 1 if i == 0 else 0
        bytes_wait(recv_rows.at[pl.ds(0, quarter - first)], rsem.at[4 + i])
        block = recv_rows[i * quarter : (i + 1) * quarter].reshape(quarter * 2 * MOST, width // 2)
        index = (iota((rows, quarter * 2 * MOST), 1) + i * quarter * 2 * MOST).astype(F32)
        take_left = jnp.where(place == index, 1.0, 0.0).astype(BF16)
        take_right = jnp.where(place + MOST == index, 1.0, 0.0).astype(BF16)
        left = left + nn(take_left, block)
        right = right + nn(take_right, block)
    xx[rows:, : width // 2] = left.astype(BF16)
    xx[rows:, width // 2 :] = right.astype(BF16)
    bytes_wait(recv_rows.at[pl.ds(0, devices - 1)], ssem.at[1])

    x0 = xx[rows:, :]
    block = 256
    for n in range(0, hidden, block):
        t = jnp.tanh(nn(x0, w1_ref[:, n : n + block]) + b1_ref[:, n : n + block])
        aa[rows:, n : n + block] = t.astype(BF16)
        u0[:, n : n + block] = 1.0 - t * t
    for n in range(0, width, block):
        cols = slice(n, n + block)
        f = nn(aa[rows:, :], w2_ref[:, cols]) + b2_ref[:, cols]
        kick = sigma_ref[:, cols] * noise_ref[:, cols].astype(F32)
        f0s[:, cols] = f
        xx[:rows, cols] = (xx[rows:, cols].astype(F32) + HEUN * f + kick).astype(BF16)
    xp = xx[:rows, :]
    for n in range(0, hidden, block):
        t = jnp.tanh(nn(xp, w1_ref[:, n : n + block]) + b1_ref[:, n : n + block])
        aa[:rows, n : n + block] = t.astype(BF16)
        u1[:, n : n + block] = 1.0 - t * t
    for n in range(0, width, block):
        cols = slice(n, n + block)
        f = nn(aa[:rows, :], w2_ref[:, cols]) + b2_ref[:, cols]
        kick = sigma_ref[:, cols] * noise_ref[:, cols].astype(F32)
        xn = xx[rows:, cols].astype(F32) + 0.5 * HEUN * (f0s[:, cols] + f) + kick
        xnb[:, cols] = xn.astype(BF16)
    resid = (obs_ref[...].astype(F32) - nn(xnb[...], c_ref[...])) * inv_ref[...]
    loglik = -0.5 * jnp.sum(resid * resid, axis=1, keepdims=True)

    peak = jnp.max(loglik, axis=0, keepdims=True)
    total = jnp.sum(jnp.exp(loglik - peak), axis=0, keepdims=True)
    norm_src[0] = jnp.where(iota((1, 128), 1) == 0, peak, total)
    exchange(2, norm_src, norm_tab, False)
    norm_tab[me] = norm_src[0]
    exchange_wait(2, norm_tab)
    table = norm_tab[...]
    peaks, totals = table[:, :, 0:1], table[:, :, 1:2]
    top = jnp.max(peaks, axis=0, keepdims=True)
    mass = jnp.sum(totals * jnp.exp(peaks - top), axis=0, keepdims=True)
    weight = jnp.exp(loglik - top[0]) / mass[0] * float(rows * devices)

    dmean = (weight * resid * inv_ref[...]).astype(BF16)
    for n in range(0, width, block):
        cols = slice(n, n + block)
        gxn = g_ref[:, cols].astype(F32) + nt(dmean, c_ref[cols, :])
        gxs[:, cols] = gxn
        gf[:rows, cols] = (0.5 * HEUN * gxn).astype(BF16)
    for n in range(0, hidden, block):
        cols = slice(n, n + block)
        one = nt(gf[:rows, :], w2_ref[cols, :]) * u1[:, cols]
        gp[:rows, cols] = one.astype(BF16)
        dots[:, cols] = jnp.sum(one, axis=0, keepdims=True)
    for n in range(0, width, block):
        cols = slice(n, n + block)
        gxn = gxs[:, cols]
        gxp = nt(gp[:rows, :], w1_ref[cols, :])
        both = gxn + gxp
        gf0 = 0.5 * HEUN * gxn + HEUN * gxp
        gf[rows:, cols] = gf0.astype(BF16)
        gxs[:, cols] = both
        d_b2 = jnp.sum(0.5 * HEUN * gxn + gf0, axis=0, keepdims=True)
        d_sigma = jnp.sum(both * noise_ref[:, cols].astype(F32), axis=0, keepdims=True)
        for j in range(block // 128):
            at = n // 128 + j
            accx[1, 1, at : at + 1, :] = d_b2[:, 128 * j : 128 * (j + 1)]
            accx[1, 2, at : at + 1, :] = d_sigma[:, 128 * j : 128 * (j + 1)]
    for n in range(0, hidden, block):
        cols = slice(n, n + block)
        zero = nt(gf[rows:, :], w2_ref[cols, :]) * u0[:, cols]
        gp[rows:, cols] = zero.astype(BF16)
        d_b1 = dots[:, cols] + jnp.sum(zero, axis=0, keepdims=True)
        for j in range(block // 128):
            at = n // 128 + j
            accx[1, 0, at : at + 1, :] = d_b1[:, 128 * j : 128 * (j + 1)]
    for n in range(0, width, block):
        cols = slice(n, n + block)
        gxs[:, cols] = gxs[:, cols] + nt(gp[rows:, :], w1_ref[cols, :])

    gx_high, gx_low = split(gxs[...])

    def give(i, carry):
        at = pl.multiple_of(i * group, group)
        onehot = jnp.where(iota((group * MOST, rows), 0) + at * MOST == flat, 1.0, 0.0).astype(BF16)
        out = nn(onehot, gx_high) + nn(onehot, gx_low)
        word, level = encode_wide(out.reshape(group, MOST, width))
        ret[pl.ds(at, group)] = jnp.concatenate([word, level], axis=1)
        return carry

    lax.fori_loop(0, devices // group, give, 0)
    exchange(3, ret, arr_ref, True)
    arr_ref[me] = ret[me]

    accx[1, 1, 4:8, :] = jnp.zeros((4, 128), F32)
    accx[1, 2, 4:8, :] = jnp.zeros((4, 128), F32)
    accx[1, pl.ds(3, chips - 3)] = jnp.zeros((chips - 3, 8, 128), F32)
    accx[0] = tn(xnb[...], dmean).reshape(chips, 8, 128)
    for n in range(0, hidden, block):
        acc2[n // 8 : (n + block) // 8] = tn(aa[:, n : n + block], gf[...]).reshape(block // 8, 8, width)

    def core_swap(i, source, target):
        swap = pltpu.make_async_remote_copy(
            src_ref=source, dst_ref=target, send_sem=ssem.at[8 + i], recv_sem=rsem.at[8 + i],
            device_id=(other,), device_id_type=MESH,
        )
        swap.start()
        return swap

    theirs = pl.ds((1 - core) * chips, chips)
    swaps = [core_swap(0, acc2.at[theirs], in2), core_swap(1, accx.at[1 - core], inx)]
    for h in range(2):
        acc1[h * chips : (h + 1) * chips] = tn(xx[...], gp[:, h * width : (h + 1) * width]).reshape(chips, 8, width)
    swaps.append(core_swap(2, acc1.at[theirs], in1))
    for swap in swaps:
        swap.wait()

    step = 4

    def prepare(i, carry):
        at = pl.multiple_of(i * step, step)
        mine = pl.ds(at, step)
        held = pl.ds(core * chips + at, step)
        one = in1[mine] + acc1[held]
        two = in2[mine] + acc2[held]
        rest = inx[mine] + accx[core, mine]
        values = (one[:, :, :384], two[:, :, :384], joined([one[:, :, 384:], two[:, :, 384:], rest]))
        for t in range(3):
            sums[t, mine] = values[t]
            enc1[t, mine] = encode_slice(values[t])
        return carry

    lax.fori_loop(0, chips // step, prepare, 0)

    plane = chips // 4
    along = []
    for k in (2, 1, 3):
        for t, (axis, _, _) in enumerate(streams):
            there = lax.rem(coordinate[axis] + k, 4)
            copy = pltpu.make_async_remote_copy(
                src_ref=enc1.at[t, pl.ds(there * plane, plane)], dst_ref=got1.at[t, k - 1],
                send_sem=s1.at[3 * t + k - 1], recv_sem=r1.at[3 * t + k - 1],
                device_id=(me + (there - coordinate[axis]) * stride[axis],), device_id_type=MESH,
            )
            copy.start()
            along.append(copy)

    exchange_wait(3, arr_ref)

    def settle(i, carry):
        at = pl.multiple_of(i * group, group)
        column = wanted_columns(inc_ref[pl.ds(at, group)])
        onehot = jnp.where(column == iota((group, MOST, rows), 2).astype(F32), 1.0, 0.0)
        onehot = onehot.reshape(group * MOST, rows).astype(BF16)
        word = arr_ref[pl.ds(at, group)]
        value = decode_wide(word[:, :16], word[:, 16:17]).reshape(group * MOST, width)
        upper, lower = split(value)
        return carry + tn(onehot, upper) + tn(onehot, lower)

    dprev[...] = lax.fori_loop(0, devices // group, settle, jnp.zeros((rows, width), F32))
    settled = pltpu.make_async_copy(dprev, dprev_hbm, lsem.at[7])
    settled.start()

    for copy in along:
        copy.wait()
    home = [coordinate[axis] * plane for axis, _, _ in streams]
    spot = [coordinate[u] * 4 + coordinate[v] for _, u, v in streams]
    for t in range(3):

        def fold(i, carry):
            at = pl.multiple_of(i * step, step)
            value = sums[t, pl.ds(home[t] + at, step)]
            for k in range(3):
                value = value + joined(decode_slice(got1[t, k, pl.ds(at, step)]))
            half[t, pl.ds(at, step)] = value
            enc2[t, pl.ds(at, step)] = encode_slice(value)
            return carry

        lax.fori_loop(0, plane // step, fold, 0)

    def over_plane(t, source, target, send_sem, recv_sem):
        axis, u, v = streams[t]
        base = core + coordinate[axis] * stride[axis]

        def send(k, carry):
            there = lax.rem(spot[t] + k, plane)
            d = base + lax.div(there, 4) * stride[u] + lax.rem(there, 4) * stride[v]
            pltpu.make_async_remote_copy(
                src_ref=source(there), dst_ref=target(k), send_sem=send_sem, recv_sem=recv_sem,
                device_id=(d,), device_id_type=MESH,
            ).start()
            return carry

        lax.fori_loop(1, plane, send, 0)

    for t in range(3):
        over_plane(t, lambda there: enc2.at[t, there], lambda k: got2.at[t, k - 1], s2.at[t], r2.at[t])
    for t in range(3):
        bytes_wait(got2.at[t], r2.at[t])
        value = half[t, spot[t]][None]
        for k in range(0, plane - 1, 5):
            value = value + jnp.sum(joined(decode_slice(got2[t, k : k + 5])), axis=0, keepdims=True)
        fin[t] = encode_slice(value)
        whole[t, home[t] + spot[t]] = fin[t, 0]
        over_plane(t, lambda there: fin.at[t, 0], lambda k: whole.at[t, home[t] + spot[t]], s3.at[t], r3.at[t])

    outs = []

    def publish(i, t, first):
        source = whole.at[t, pl.ds(first, plane)]
        target = all_hbm.at[core, t, pl.ds(first, plane)]
        keep = pltpu.make_async_copy(source, target, out_sem.at[i])
        give = pltpu.make_async_remote_copy(
            src_ref=source, dst_ref=target, send_sem=s5.at[i], recv_sem=r5.at[i],
            device_id=(other,), device_id_type=MESH,
        )
        keep.start()
        give.start()
        outs.append(keep)
        outs.append(give)

    along = []
    for t, (axis, _, _) in enumerate(streams):
        bytes_wait(got2.at[t], r3.at[t])
        for k in (2, 1, 3):
            there = lax.rem(coordinate[axis] + k, 4)
            held = whole.at[t, pl.ds(home[t], plane)]
            copy = pltpu.make_async_remote_copy(
                src_ref=held, dst_ref=held, send_sem=s4.at[3 * t + k - 1], recv_sem=r4.at[3 * t + k - 1],
                device_id=(me + (there - coordinate[axis]) * stride[axis],), device_id_type=MESH,
            )
            copy.start()
            along.append((t, k, copy))
        publish(t, t, home[t])
    for t, k, copy in along:
        copy.wait_recv()
        first = lax.rem(coordinate[streams[t][0]] + 4 - k, 4) * plane
        publish(3 + 3 * t + k - 1, t, first)
    for t, k, copy in along:
        copy.wait_send()
    for t in range(3):
        bytes_wait(got2.at[t], s2.at[t])
        bytes_wait(got2.at[t], s3.at[t])
    for copy in outs:
        copy.wait()
    settled.wait()


def finish_kernel(dp_ref, all_ref, dprev_ref, dw1_ref, dw2_ref, dc_ref, db1_ref, db2_ref, dsigma_ref):
    i = pl.program_id(0)
    step = all_ref.shape[2]
    width = dprev_ref.shape[1]
    dprev_ref[...] = dp_ref[...]
    for core in range(2):
        first, second, third = (decode_slice(all_ref[core, t]) for t in range(3))
        for b in range(4):
            one = first[b] if b < 3 else third[0]
            two = second[b] if b < 3 else third[1]
            at = core * width + 128 * b
            dw1_ref[:, at : at + 128] = one.reshape(step * 8, 128)
            dw2_ref[core, :, 128 * b : 128 * (b + 1)] = two.reshape(step * 8, 128)
        rest = third[2]
        if core == 0:
            dc_ref[...] = rest.reshape(step * 8, 128)
        else:

            @pl.when(i == 0)
            def _():
                db1_ref[...] = rest[0]
                db2_ref[...] = rest[1, :4]
                dsigma_ref[...] = rest[2, :4]


def per_device(x_prev, anc_owner, anc_row, noise, g_new, obs, w1, b1, w2, b2, c_obs, inv_scale, sigma):
    devices = lax.axis_size("particle")
    chips = devices // 2
    plane = chips // 4
    rows, width = x_prev.shape
    hidden = w1.shape[1]
    vmem = pl.BlockSpec(memory_space=pltpu.VMEM)
    anywhere = pl.BlockSpec(memory_space=pl.ANY)
    dma = pltpu.SemaphoreType.DMA
    d_prev, sums = pl.pallas_call(
        functools.partial(main_kernel, devices),
        out_shape=(
            jax.ShapeDtypeStruct((rows, width), F32),
            jax.ShapeDtypeStruct((2, 3, chips, 13, 128), I32),
        ),
        in_specs=[anywhere, vmem, vmem, anywhere, anywhere, anywhere, anywhere, vmem, anywhere, vmem, anywhere, vmem, vmem],
        out_specs=(anywhere, anywhere),
        scratch_shapes=[
            pltpu.VMEM((rows, width), BF16),
            pltpu.VMEM((rows, width), BF16),
            pltpu.VMEM((rows, width), BF16),
            pltpu.VMEM((rows, 128), BF16),
            pltpu.VMEM((width, hidden), BF16),
            pltpu.VMEM((hidden, width), BF16),
            pltpu.VMEM((width, 128), BF16),
            pltpu.VMEM((rows, width), F32),
            pltpu.VMEM((devices, 1, 128), F32),
            pltpu.VMEM((devices, 17, 128), I32),
            pltpu.VMEM((devices, 1, 128), F32),
            pltpu.VMEM((devices, 128), F32),
            pltpu.VMEM((devices, 2 * MOST, width // 2), BF16),
            pltpu.VMEM((devices, 2 * MOST, width // 2), BF16),
            pltpu.VMEM((1, 1, 128), F32),
            pltpu.VMEM((devices, 1, 128), F32),
            pltpu.VMEM((devices, 17, 128), I32),
            pltpu.VMEM((2 * rows, width), BF16),
            pltpu.VMEM((2 * rows, hidden), BF16),
            pltpu.VMEM((2 * rows, width), BF16),
            pltpu.VMEM((2 * rows, hidden), BF16),
            pltpu.VMEM((rows, hidden), F32),
            pltpu.VMEM((rows, hidden), F32),
            pltpu.VMEM((rows, width), BF16),
            pltpu.VMEM((rows, width), F32),
            pltpu.VMEM((rows, width), F32),
            pltpu.VMEM((1, hidden), F32),
            pltpu.VMEM((devices, 8, width), F32),
            pltpu.VMEM((devices, 8, width), F32),
            pltpu.VMEM((2, chips, 8, 128), F32),
            pltpu.VMEM((chips, 8, width), F32),
            pltpu.VMEM((chips, 8, width), F32),
            pltpu.VMEM((chips, 8, 128), F32),
            pltpu.VMEM((3, chips, 8, 384), F32),
            pltpu.VMEM((3, chips, 13, 128), I32),
            pltpu.VMEM((3, 3, plane, 13, 128), I32),
            pltpu.VMEM((3, plane, 8, 384), F32),
            pltpu.VMEM((3, plane, 13, 128), I32),
            pltpu.VMEM((3, plane - 1, 13, 128), I32),
            pltpu.VMEM((3, 1, 13, 128), I32),
            pltpu.VMEM((3, chips, 13, 128), I32),
            dma((12,)), dma((12,)), dma((8,)),
            dma((9,)), dma((9,)), dma((3,)), dma((3,)), dma((3,)), dma((3,)), dma((9,)), dma((9,)),
            dma((12,)), dma((12,)), dma((12,)),
        ],
        compiler_params=pltpu.CompilerParams(collective_id=0, has_side_effects=True, vmem_limit_bytes=58 * 2**20),
        name="heun_step",
    )(
        x_prev, anc_owner.reshape(1, rows), anc_row.reshape(1, rows), noise, g_new, obs,
        w1, b1.reshape(1, hidden), w2, b2.reshape(1, width), c_obs, inv_scale.reshape(1, -1), sigma.reshape(1, width),
    )
    step = 8
    lines = step * 8
    d_prev, d_w1, d_w2, d_c, d_b1, d_b2, d_sigma = pl.pallas_call(
        finish_kernel,
        grid=(chips // step,),
        out_shape=(
            jax.ShapeDtypeStruct((rows, width), F32),
            jax.ShapeDtypeStruct((width, hidden), F32),
            jax.ShapeDtypeStruct((2, hidden // 2, width), F32),
            jax.ShapeDtypeStruct((width, 128), F32),
            jax.ShapeDtypeStruct((hidden // 128, 128), F32),
            jax.ShapeDtypeStruct((width // 128, 128), F32),
            jax.ShapeDtypeStruct((width // 128, 128), F32),
        ),
        in_specs=[
            pl.BlockSpec((lines, width), lambda i: (i, 0)),
            pl.BlockSpec((2, 3, step, 13, 128), lambda i: (0, 0, i, 0, 0)),
        ],
        out_specs=(
            pl.BlockSpec((lines, width), lambda i: (i, 0)),
            pl.BlockSpec((lines, hidden), lambda i: (i, 0)),
            pl.BlockSpec((2, lines, width), lambda i: (0, i, 0)),
            pl.BlockSpec((lines, 128), lambda i: (i, 0)),
            pl.BlockSpec((hidden // 128, 128), lambda i: (0, 0)),
            pl.BlockSpec((width // 128, 128), lambda i: (0, 0)),
            pl.BlockSpec((width // 128, 128), lambda i: (0, 0)),
        ),
        compiler_params=pltpu.CompilerParams(vmem_limit_bytes=58 * 2**20),
        name="place_results",
    )(d_prev, sums)
    return (
        d_prev, d_w1, d_b1.reshape(hidden), d_w2.reshape(hidden, width), d_b2.reshape(width), d_c, d_sigma.reshape(width),
    )


def solution(mesh):
    split_rows = P("particle", None)
    return jax.shard_map(
        per_device,
        mesh=mesh,
        in_specs=(split_rows, split_rows, P("particle"), split_rows, split_rows, split_rows) + (P(),) * 7,
        out_specs=(split_rows, P(), P(), P(), P(), P(), P()),
        check_vma=False,
    )
```

```python
import functools

import jax
import jax.numpy as jnp
from jax import lax
from jax.experimental import pallas as pl
from jax.experimental.pallas import tpu as pltpu
from jax.sharding import PartitionSpec as P

MESH = pl.DeviceIdType.MESH
HEUN = 0.25
F32 = jnp.float32
BF16 = jnp.bfloat16
I32 = jnp.int32
HOP, BACK = 11, 35
MOST = 8
LOGSTEP = 65536.0
TOP = 32767.0


def nn(left, right):
    return jnp.dot(left, right, preferred_element_type=F32)


def nt(left, right):
    return lax.dot_general(left, right, (((1,), (1,)), ((), ())), preferred_element_type=F32)


def tn(left, right):
    return lax.dot_general(left, right, (((0,), (0,)), ((), ())), preferred_element_type=F32)


def iota(shape, dim):
    return lax.broadcasted_iota(I32, shape, dim)


def split(value):
    high = value.astype(BF16)
    return high, (value - high.astype(F32)).astype(BF16)


def encode(value):
    peak = jnp.max(jnp.max(jnp.abs(value), axis=2, keepdims=True), axis=1, keepdims=True)
    level = jnp.ceil(jnp.log(jnp.maximum(peak, 1e-30)) * LOGSTEP).astype(I32)
    scale = TOP * jnp.exp(level.astype(F32) * (-1.0 / LOGSTEP))
    code = jnp.round(value * scale).astype(I32)
    return code, jnp.broadcast_to(level, (value.shape[0], 1, 128))


def pack(low, high):
    return jnp.bitwise_or(jnp.left_shift(high, 16), jnp.bitwise_and(low, 0xFFFF))


def unpack(word):
    low = jnp.right_shift(jnp.left_shift(word, 16), 16)
    return low.astype(F32), jnp.right_shift(word, 16).astype(F32)


def encode_wide(value):
    code, level = encode(value)
    word = pack(code[:, :, :256], code[:, :, 256:])
    return jnp.concatenate([word[:, :, :128], word[:, :, 128:]], axis=1), level


def unscale(level):
    return jnp.exp(level.astype(F32) * (1.0 / LOGSTEP)) * (1.0 / TOP)


def decode_wide(word, level):
    scale = unscale(level)
    low0, high0 = unpack(word[:, :8])
    low1, high1 = unpack(word[:, 8:])
    return jnp.concatenate([low0 * scale, low1 * scale, high0 * scale, high1 * scale], axis=2)


def encode_slice(value):
    codes, levels = zip(*(encode(value[:, :, 128 * b : 128 * (b + 1)]) for b in range(3)))
    lane = iota((value.shape[0], 1, 128), 2)
    level = jnp.where(lane == 0, levels[0], jnp.where(lane == 1, levels[1], levels[2]))
    return jnp.concatenate([pack(codes[0], codes[1]), pack(codes[2][:, :4], codes[2][:, 4:]), level], axis=1)


def decode_slice(word):
    scale = unscale(word[:, 12:13])
    low, high = unpack(word[:, :8])
    top, bottom = unpack(word[:, 8:12])
    last = jnp.concatenate([top, bottom], axis=1)
    return low * scale[:, :, 0:1], high * scale[:, :, 1:2], last * scale[:, :, 2:3]


def joined(blocks):
    return jnp.concatenate(blocks, axis=2)


def wanted_columns(table):
    shape = (1, MOST, 128)
    lane, sub = iota(shape, 2), iota(shape, 1)
    one = jnp.where((lane == sub) | (lane == sub + 2 * MOST), 1.0, 0.0)
    weight = jnp.where(lane == sub + MOST, 256.0, one)
    return jnp.sum(table * weight, axis=2, keepdims=True) - 1.0


def bytes_wait(ref, semaphore):
    pltpu.make_async_copy(ref, ref, semaphore).wait()


def main_kernel(
    devices,
    x_hbm, owner_ref, row_ref, noise_hbm, g_hbm, obs_hbm, w1_hbm, b1_ref, w2_hbm, b2_ref, c_hbm, inv_ref, sigma_ref,
    dprev_hbm, all_hbm,
    x_ref, noise_ref, g_ref, obs_ref, w1_ref, w2_ref, c_ref, dprev, inc_ref, arr_ref,
    wtab, wrow, send_rows, recv_rows, norm_src, norm_tab, ret, xx, aa, gf, gp, u0, u1, xnb, f0s, gxs, dots,
    acc1, acc2, accx, in1, in2, inx, sums, enc1, got1, half, enc2, got2, fin, whole,
    ssem, rsem, lsem, s1, r1, s2, r2, s3, r3, s4, r4, s5, r5, out_sem,
):
    me = lax.axis_index("particle")
    rows, width = x_ref.shape
    hidden = w1_ref.shape[1]
    chips = devices // 2
    core = lax.rem(me, 2)
    other = me + 1 - 2 * core
    stride = {"x": 2, "z": 8, "y": 32}
    coordinate = {axis: lax.rem(lax.div(me, by), 4) for axis, by in stride.items()}
    streams = (("x", "y", "z"), ("z", "x", "y"), ("y", "z", "x"))

    barrier = pltpu.get_barrier_semaphore()

    def greet(k, carry):
        pl.semaphore_signal(barrier, inc=1, device_id=(lax.rem(me + k, devices),), device_id_type=MESH)
        return carry

    lax.fori_loop(1, devices, greet, 0)
    loads = [
        pltpu.make_async_copy(source, target, lsem.at[i])
        for i, (source, target) in enumerate(
            (
                (x_hbm, x_ref),
                (w1_hbm, w1_ref),
                (w2_hbm, w2_ref),
                (noise_hbm, noise_ref),
                (g_hbm, g_ref),
                (obs_hbm, obs_ref),
                (c_hbm, c_ref),
            )
        )
    ]
    for load in loads:
        load.start()

    owner = owner_ref[...]
    row = row_ref[...]
    named = jnp.where(iota((devices, rows), 0) == owner, 1.0, 0.0)
    named_b = named.astype(BF16)
    earlier = jnp.where(iota((rows, rows), 0) < iota((rows, rows), 1), 1.0, 0.0).astype(BF16)
    slot = jnp.sum(nn(named_b, earlier) * named, axis=0, keepdims=True)
    part = iota((128, rows), 0)
    low = jnp.bitwise_and(row, 255).astype(F32)
    high = jnp.right_shift(row, 8).astype(F32)
    value = jnp.where(part < MOST, low, jnp.where(part < 2 * MOST, high, jnp.where(part < 3 * MOST, 1.0, 0.0)))
    value = jnp.where(jnp.bitwise_and(part, MOST - 1).astype(F32) == slot, value, 0.0)
    wrow[...] = nt(named_b, value.astype(BF16))

    def spread(d, carry):
        wtab[d] = wrow[pl.ds(d, 1), :]
        return carry

    lax.fori_loop(0, devices, spread, 0, unroll=8)
    eye = jnp.where(iota((rows, rows), 0) == iota((rows, rows), 1), 1.0, 0.0).astype(BF16)
    turn = jnp.bitwise_and((me - owner + devices) * BACK, devices - 1)
    pair = jnp.where(part == 0, turn.astype(F32), jnp.where(part == 1, slot, 0.0)).astype(BF16)
    turned = nt(eye, pair)
    place = turned[:, 0:1] * (2 * MOST) + turned[:, 1:2]
    flat = owner * MOST + slot.astype(I32)

    pl.semaphore_wait(barrier, devices - 1)

    def exchange(stage, source, target, per_partner, by_turn=False):
        def send(k, carry):
            d = lax.rem(me + lax.rem(HOP * k, devices), devices)
            pltpu.make_async_remote_copy(
                src_ref=source.at[d] if per_partner else source.at[0],
                dst_ref=target.at[k] if by_turn else target.at[me],
                send_sem=ssem.at[stage],
                recv_sem=rsem.at[4 + lax.div(k, devices // 4)] if by_turn else rsem.at[stage],
                device_id=(d,),
                device_id_type=MESH,
            ).start()
            return carry

        lax.fori_loop(1, devices, send, 0)

    def exchange_wait(stage, target):
        most = target.at[pl.ds(0, devices - 1)]
        bytes_wait(most, ssem.at[stage])
        bytes_wait(most, rsem.at[stage])

    exchange(0, wtab, inc_ref, True)
    inc_ref[me] = wtab[me]
    exchange_wait(0, inc_ref)

    group = 16

    def gather(i, carry):
        at = pl.multiple_of(i * group, group)
        column = wanted_columns(inc_ref[pl.ds(at, group)])
        onehot = jnp.where(column == iota((group, MOST, rows), 2).astype(F32), 1.0, 0.0)
        out = nn(onehot.reshape(group * MOST, rows).astype(BF16), x_ref[...])
        halves = jnp.concatenate(
            [out[:, : width // 2].reshape(group, MOST, width // 2), out[:, width // 2 :].reshape(group, MOST, width // 2)],
            axis=1,
        )
        send_rows[pl.ds(at, group)] = halves.astype(BF16)
        return carry

    loads[0].wait()
    lax.fori_loop(0, devices // group, gather, 0)
    exchange(1, send_rows, recv_rows, True, by_turn=True)
    recv_rows[0] = send_rows[me]
    for load in loads[1:]:
        load.wait()

    left = jnp.zeros((rows, width // 2), F32)
    right = left
    quarter = devices // 4
    for i in range(4):
        first = 1 if i == 0 else 0
        bytes_wait(recv_rows.at[pl.ds(0, quarter - first)], rsem.at[4 + i])
        block = recv_rows[i * quarter : (i + 1) * quarter].reshape(quarter * 2 * MOST, width // 2)
        index = (iota((rows, quarter * 2 * MOST), 1) + i * quarter * 2 * MOST).astype(F32)
        take_left = jnp.where(place == index, 1.0, 0.0).astype(BF16)
        take_right = jnp.where(place + MOST == index, 1.0, 0.0).astype(BF16)
        left = left + nn(take_left, block)
        right = right + nn(take_right, block)
    xx[rows:, : width // 2] = left.astype(BF16)
    xx[rows:, width // 2 :] = right.astype(BF16)
    bytes_wait(recv_rows.at[pl.ds(0, devices - 1)], ssem.at[1])

    x0 = xx[rows:, :]
    block = 256
    for n in range(0, hidden, block):
        t = jnp.tanh(nn(x0, w1_ref[:, n : n + block]) + b1_ref[:, n : n + block])
        aa[rows:, n : n + block] = t.astype(BF16)
        u0[:, n : n + block] = 1.0 - t * t
    for n in range(0, width, block):
        cols = slice(n, n + block)
        f = nn(aa[rows:, :], w2_ref[:, cols]) + b2_ref[:, cols]
        kick = sigma_ref[:, cols] * noise_ref[:, cols].astype(F32)
        f0s[:, cols] = f
        xx[:rows, cols] = (xx[rows:, cols].astype(F32) + HEUN * f + kick).astype(BF16)
    xp = xx[:rows, :]
    for n in range(0, hidden, block):
        t = jnp.tanh(nn(xp, w1_ref[:, n : n + block]) + b1_ref[:, n : n + block])
        aa[:rows, n : n + block] = t.astype(BF16)
        u1[:, n : n + block] = 1.0 - t * t
    for n in range(0, width, block):
        cols = slice(n, n + block)
        f = nn(aa[:rows, :], w2_ref[:, cols]) + b2_ref[:, cols]
        kick = sigma_ref[:, cols] * noise_ref[:, cols].astype(F32)
        xn = xx[rows:, cols].astype(F32) + 0.5 * HEUN * (f0s[:, cols] + f) + kick
        xnb[:, cols] = xn.astype(BF16)
    resid = (obs_ref[...].astype(F32) - nn(xnb[...], c_ref[...])) * inv_ref[...]
    loglik = -0.5 * jnp.sum(resid * resid, axis=1, keepdims=True)

    peak = jnp.max(loglik, axis=0, keepdims=True)
    total = jnp.sum(jnp.exp(loglik - peak), axis=0, keepdims=True)
    norm_src[0] = jnp.where(iota((1, 128), 1) == 0, peak, total)
    exchange(2, norm_src, norm_tab, False)
    norm_tab[me] = norm_src[0]
    exchange_wait(2, norm_tab)
    table = norm_tab[...]
    peaks, totals = table[:, :, 0:1], table[:, :, 1:2]
    top = jnp.max(peaks, axis=0, keepdims=True)
    mass = jnp.sum(totals * jnp.exp(peaks - top), axis=0, keepdims=True)
    weight = jnp.exp(loglik - top[0]) / mass[0] * float(rows * devices)

    dmean = (weight * resid * inv_ref[...]).astype(BF16)
    for n in range(0, width, block):
        cols = slice(n, n + block)
        gxn = g_ref[:, cols].astype(F32) + nt(dmean, c_ref[cols, :])
        gxs[:, cols] = gxn
        gf[:rows, cols] = (0.5 * HEUN * gxn).astype(BF16)
    for n in range(0, hidden, block):
        cols = slice(n, n + block)
        one = nt(gf[:rows, :], w2_ref[cols, :]) * u1[:, cols]
        gp[:rows, cols] = one.astype(BF16)
        dots[:, cols] = jnp.sum(one, axis=0, keepdims=True)
    for n in range(0, width, block):
        cols = slice(n, n + block)
        gxn = gxs[:, cols]
        gxp = nt(gp[:rows, :], w1_ref[cols, :])
        both = gxn + gxp
        gf0 = 0.5 * HEUN * gxn + HEUN * gxp
        gf[rows:, cols] = gf0.astype(BF16)
        gxs[:, cols] = both
        d_b2 = jnp.sum(0.5 * HEUN * gxn + gf0, axis=0, keepdims=True)
        d_sigma = jnp.sum(both * noise_ref[:, cols].astype(F32), axis=0, keepdims=True)
        for j in range(block // 128):
            at = n // 128 + j
            accx[1, 1, at : at + 1, :] = d_b2[:, 128 * j : 128 * (j + 1)]
            accx[1, 2, at : at + 1, :] = d_sigma[:, 128 * j : 128 * (j + 1)]
    def core_swap(i, source, target):
        swap = pltpu.make_async_remote_copy(
            src_ref=source, dst_ref=target, send_sem=ssem.at[8 + i], recv_sem=rsem.at[8 + i],
            device_id=(other,), device_id_type=MESH,
        )
        swap.start()
        return swap

    theirs = pl.ds((1 - core) * chips, chips)
    accx[0] = tn(xnb[...], dmean).reshape(chips, 8, 128)
    for n in range(0, hidden, block):
        acc2[n // 8 : (n + block) // 8] = tn(aa[:, n : n + block], gf[...]).reshape(block // 8, 8, width)

    swaps = [core_swap(0, acc2.at[theirs], in2)]
    for n in range(0, hidden, block):
        cols = slice(n, n + block)
        zero = nt(gf[rows:, :], w2_ref[cols, :]) * u0[:, cols]
        gp[rows:, cols] = zero.astype(BF16)
        d_b1 = dots[:, cols] + jnp.sum(zero, axis=0, keepdims=True)
        for j in range(block // 128):
            at = n // 128 + j
            accx[1, 0, at : at + 1, :] = d_b1[:, 128 * j : 128 * (j + 1)]
    accx[1, 1, 4:8, :] = jnp.zeros((4, 128), F32)
    accx[1, 2, 4:8, :] = jnp.zeros((4, 128), F32)
    accx[1, pl.ds(3, chips - 3)] = jnp.zeros((chips - 3, 8, 128), F32)
    swaps.append(core_swap(1, accx.at[1 - core], inx))
    for h in range(2):
        acc1[h * chips : (h + 1) * chips] = tn(xx[...], gp[:, h * width : (h + 1) * width]).reshape(chips, 8, width)
    swaps.append(core_swap(2, acc1.at[theirs], in1))
    for n in range(0, width, block):
        cols = slice(n, n + block)
        gxs[:, cols] = gxs[:, cols] + nt(gp[rows:, :], w1_ref[cols, :])


    gx_high, gx_low = split(gxs[...])

    def give(i, carry):
        at = pl.multiple_of(i * group, group)
        onehot = jnp.where(iota((group * MOST, rows), 0) + at * MOST == flat, 1.0, 0.0).astype(BF16)
        out = nn(onehot, gx_high) + nn(onehot, gx_low)
        word, level = encode_wide(out.reshape(group, MOST, width))
        ret[pl.ds(at, group)] = jnp.concatenate([word, level], axis=1)
        return carry

    lax.fori_loop(0, devices // group, give, 0)
    for swap in swaps:
        swap.wait()

    step = 4

    def prepare(i, carry):
        at = pl.multiple_of(i * step, step)
        mine = pl.ds(at, step)
        held = pl.ds(core * chips + at, step)
        one = in1[mine] + acc1[held]
        two = in2[mine] + acc2[held]
        rest = inx[mine] + accx[core, mine]
        values = (one[:, :, :384], two[:, :, :384], joined([one[:, :, 384:], two[:, :, 384:], rest]))
        for t in range(3):
            sums[t, mine] = values[t]
            enc1[t, mine] = encode_slice(values[t])
        return carry

    lax.fori_loop(0, chips // step, prepare, 0)

    plane = chips // 4
    along = []
    for k in (2, 1, 3):
        for t, (axis, _, _) in enumerate(streams):
            there = lax.rem(coordinate[axis] + k, 4)
            copy = pltpu.make_async_remote_copy(
                src_ref=enc1.at[t, pl.ds(there * plane, plane)], dst_ref=got1.at[t, k - 1],
                send_sem=s1.at[3 * t + k - 1], recv_sem=r1.at[3 * t + k - 1],
                device_id=(me + (there - coordinate[axis]) * stride[axis],), device_id_type=MESH,
            )
            copy.start()
            along.append((t, copy))

    exchange(3, ret, arr_ref, True)
    arr_ref[me] = ret[me]

    home = [coordinate[axis] * plane for axis, _, _ in streams]
    spot = [coordinate[u] * 4 + coordinate[v] for _, u, v in streams]
    def over_plane(t, source, target, send_sem, recv_sem):
        axis, u, v = streams[t]
        base = core + coordinate[axis] * stride[axis]

        def send(k, carry):
            there = lax.rem(spot[t] + k, plane)
            d = base + lax.div(there, 4) * stride[u] + lax.rem(there, 4) * stride[v]
            pltpu.make_async_remote_copy(
                src_ref=source(there), dst_ref=target(k), send_sem=send_sem, recv_sem=recv_sem,
                device_id=(d,), device_id_type=MESH,
            ).start()
            return carry

        lax.fori_loop(1, plane, send, 0)

    for t in range(3):
        for stream, copy in along:
            if stream == t:
                copy.wait()

        def fold(i, carry):
            at = pl.multiple_of(i * step, step)
            value = sums[t, pl.ds(home[t] + at, step)]
            for k in range(3):
                value = value + joined(decode_slice(got1[t, k, pl.ds(at, step)]))
            half[t, pl.ds(at, step)] = value
            enc2[t, pl.ds(at, step)] = encode_slice(value)
            return carry

        lax.fori_loop(0, plane // step, fold, 0)
        over_plane(t, lambda there: enc2.at[t, there], lambda k: got2.at[t, k - 1], s2.at[t], r2.at[t])
    for t in range(3):
        bytes_wait(got2.at[t], r2.at[t])
        value = half[t, spot[t]][None]
        for k in range(0, plane - 1, 5):
            value = value + jnp.sum(joined(decode_slice(got2[t, k : k + 5])), axis=0, keepdims=True)
        fin[t] = encode_slice(value)
        whole[t, home[t] + spot[t]] = fin[t, 0]
        over_plane(t, lambda there: fin.at[t, 0], lambda k: whole.at[t, home[t] + spot[t]], s3.at[t], r3.at[t])

    outs = []

    def publish(i, t, first):
        source = whole.at[t, pl.ds(first, plane)]
        target = all_hbm.at[core, t, pl.ds(first, plane)]
        keep = pltpu.make_async_copy(source, target, out_sem.at[i])
        give = pltpu.make_async_remote_copy(
            src_ref=source, dst_ref=target, send_sem=s5.at[i], recv_sem=r5.at[i],
            device_id=(other,), device_id_type=MESH,
        )
        keep.start()
        give.start()
        outs.append(keep)
        outs.append(give)

    along = []
    for t, (axis, _, _) in enumerate(streams):
        bytes_wait(got2.at[t], r3.at[t])
        for k in (2, 1, 3):
            there = lax.rem(coordinate[axis] + k, 4)
            held = whole.at[t, pl.ds(home[t], plane)]
            copy = pltpu.make_async_remote_copy(
                src_ref=held, dst_ref=held, send_sem=s4.at[3 * t + k - 1], recv_sem=r4.at[3 * t + k - 1],
                device_id=(me + (there - coordinate[axis]) * stride[axis],), device_id_type=MESH,
            )
            copy.start()
            along.append((t, k, copy))
        publish(t, t, home[t])
    exchange_wait(3, arr_ref)

    def settle(i, carry):
        at = pl.multiple_of(i * group, group)
        column = wanted_columns(inc_ref[pl.ds(at, group)])
        onehot = jnp.where(column == iota((group, MOST, rows), 2).astype(F32), 1.0, 0.0)
        onehot = onehot.reshape(group * MOST, rows).astype(BF16)
        word = arr_ref[pl.ds(at, group)]
        value = decode_wide(word[:, :16], word[:, 16:17]).reshape(group * MOST, width)
        upper, lower = split(value)
        return carry + tn(onehot, upper) + tn(onehot, lower)

    dprev[...] = lax.fori_loop(0, devices // group, settle, jnp.zeros((rows, width), F32))
    settled = pltpu.make_async_copy(dprev, dprev_hbm, lsem.at[7])
    settled.start()

    for t, k, copy in along:
        copy.wait_recv()
        first = lax.rem(coordinate[streams[t][0]] + 4 - k, 4) * plane
        publish(3 + 3 * t + k - 1, t, first)
    for t, k, copy in along:
        copy.wait_send()
    for t in range(3):
        bytes_wait(got2.at[t], s2.at[t])
        bytes_wait(got2.at[t], s3.at[t])
    for copy in outs:
        copy.wait()
    settled.wait()


def finish_kernel(dp_ref, all_ref, dprev_ref, dw1_ref, dw2_ref, dc_ref, db1_ref, db2_ref, dsigma_ref):
    i = pl.program_id(0)
    step = all_ref.shape[2]
    width = dprev_ref.shape[1]
    dprev_ref[...] = dp_ref[...]
    for core in range(2):
        first, second, third = (decode_slice(all_ref[core, t]) for t in range(3))
        for b in range(4):
            one = first[b] if b < 3 else third[0]
            two = second[b] if b < 3 else third[1]
            at = core * width + 128 * b
            dw1_ref[:, at : at + 128] = one.reshape(step * 8, 128)
            dw2_ref[core, :, 128 * b : 128 * (b + 1)] = two.reshape(step * 8, 128)
        rest = third[2]
        if core == 0:
            dc_ref[...] = rest.reshape(step * 8, 128)
        else:

            @pl.when(i == 0)
            def _():
                db1_ref[...] = rest[0]
                db2_ref[...] = rest[1, :4]
                dsigma_ref[...] = rest[2, :4]


def per_device(x_prev, anc_owner, anc_row, noise, g_new, obs, w1, b1, w2, b2, c_obs, inv_scale, sigma):
    devices = lax.axis_size("particle")
    chips = devices // 2
    plane = chips // 4
    rows, width = x_prev.shape
    hidden = w1.shape[1]
    vmem = pl.BlockSpec(memory_space=pltpu.VMEM)
    anywhere = pl.BlockSpec(memory_space=pl.ANY)
    dma = pltpu.SemaphoreType.DMA
    d_prev, sums = pl.pallas_call(
        functools.partial(main_kernel, devices),
        out_shape=(
            jax.ShapeDtypeStruct((rows, width), F32),
            jax.ShapeDtypeStruct((2, 3, chips, 13, 128), I32),
        ),
        in_specs=[anywhere, vmem, vmem, anywhere, anywhere, anywhere, anywhere, vmem, anywhere, vmem, anywhere, vmem, vmem],
        out_specs=(anywhere, anywhere),
        scratch_shapes=[
            pltpu.VMEM((rows, width), BF16),
            pltpu.VMEM((rows, width), BF16),
            pltpu.VMEM((rows, width), BF16),
            pltpu.VMEM((rows, 128), BF16),
            pltpu.VMEM((width, hidden), BF16),
            pltpu.VMEM((hidden, width), BF16),
            pltpu.VMEM((width, 128), BF16),
            pltpu.VMEM((rows, width), F32),
            pltpu.VMEM((devices, 1, 128), F32),
            pltpu.VMEM((devices, 17, 128), I32),
            pltpu.VMEM((devices, 1, 128), F32),
            pltpu.VMEM((devices, 128), F32),
            pltpu.VMEM((devices, 2 * MOST, width // 2), BF16),
            pltpu.VMEM((devices, 2 * MOST, width // 2), BF16),
            pltpu.VMEM((1, 1, 128), F32),
            pltpu.VMEM((devices, 1, 128), F32),
            pltpu.VMEM((devices, 17, 128), I32),
            pltpu.VMEM((2 * rows, width), BF16),
            pltpu.VMEM((2 * rows, hidden), BF16),
            pltpu.VMEM((2 * rows, width), BF16),
            pltpu.VMEM((2 * rows, hidden), BF16),
            pltpu.VMEM((rows, hidden), F32),
            pltpu.VMEM((rows, hidden), F32),
            pltpu.VMEM((rows, width), BF16),
            pltpu.VMEM((rows, width), F32),
            pltpu.VMEM((rows, width), F32),
            pltpu.VMEM((1, hidden), F32),
            pltpu.VMEM((devices, 8, width), F32),
            pltpu.VMEM((devices, 8, width), F32),
            pltpu.VMEM((2, chips, 8, 128), F32),
            pltpu.VMEM((chips, 8, width), F32),
            pltpu.VMEM((chips, 8, width), F32),
            pltpu.VMEM((chips, 8, 128), F32),
            pltpu.VMEM((3, chips, 8, 384), F32),
            pltpu.VMEM((3, chips, 13, 128), I32),
            pltpu.VMEM((3, 3, plane, 13, 128), I32),
            pltpu.VMEM((3, plane, 8, 384), F32),
            pltpu.VMEM((3, plane, 13, 128), I32),
            pltpu.VMEM((3, plane - 1, 13, 128), I32),
            pltpu.VMEM((3, 1, 13, 128), I32),
            pltpu.VMEM((3, chips, 13, 128), I32),
            dma((12,)), dma((12,)), dma((8,)),
            dma((9,)), dma((9,)), dma((3,)), dma((3,)), dma((3,)), dma((3,)), dma((9,)), dma((9,)),
            dma((12,)), dma((12,)), dma((12,)),
        ],
        compiler_params=pltpu.CompilerParams(collective_id=0, has_side_effects=True, vmem_limit_bytes=58 * 2**20),
        name="heun_step",
    )(
        x_prev, anc_owner.reshape(1, rows), anc_row.reshape(1, rows), noise, g_new, obs,
        w1, b1.reshape(1, hidden), w2, b2.reshape(1, width), c_obs, inv_scale.reshape(1, -1), sigma.reshape(1, width),
    )
    step = 32
    lines = step * 8
    d_prev, d_w1, d_w2, d_c, d_b1, d_b2, d_sigma = pl.pallas_call(
        finish_kernel,
        grid=(chips // step,),
        out_shape=(
            jax.ShapeDtypeStruct((rows, width), F32),
            jax.ShapeDtypeStruct((width, hidden), F32),
            jax.ShapeDtypeStruct((2, hidden // 2, width), F32),
            jax.ShapeDtypeStruct((width, 128), F32),
            jax.ShapeDtypeStruct((hidden // 128, 128), F32),
            jax.ShapeDtypeStruct((width // 128, 128), F32),
            jax.ShapeDtypeStruct((width // 128, 128), F32),
        ),
        in_specs=[
            pl.BlockSpec((lines, width), lambda i: (i, 0)),
            pl.BlockSpec((2, 3, step, 13, 128), lambda i: (0, 0, i, 0, 0)),
        ],
        out_specs=(
            pl.BlockSpec((lines, width), lambda i: (i, 0)),
            pl.BlockSpec((lines, hidden), lambda i: (i, 0)),
            pl.BlockSpec((2, lines, width), lambda i: (0, i, 0)),
            pl.BlockSpec((lines, 128), lambda i: (i, 0)),
            pl.BlockSpec((hidden // 128, 128), lambda i: (0, 0)),
            pl.BlockSpec((width // 128, 128), lambda i: (0, 0)),
            pl.BlockSpec((width // 128, 128), lambda i: (0, 0)),
        ),
        compiler_params=pltpu.CompilerParams(vmem_limit_bytes=58 * 2**20),
        name="place_results",
    )(d_prev, sums)
    return (
        d_prev, d_w1, d_b1.reshape(hidden), d_w2.reshape(hidden, width), d_b2.reshape(width), d_c, d_sigma.reshape(width),
    )


def solution(mesh):
    split_rows = P("particle", None)
    return jax.shard_map(
        per_device,
        mesh=mesh,
        in_specs=(split_rows, split_rows, P("particle"), split_rows, split_rows, split_rows) + (P(),) * 7,
        out_specs=(split_rows, P(), P(), P(), P(), P(), P()),
        check_vma=False,
    )
```

```python
import functools

import jax
import jax.numpy as jnp
from jax import lax
from jax.experimental import pallas as pl
from jax.experimental.pallas import tpu as pltpu
from jax.sharding import PartitionSpec as P

MESH = pl.DeviceIdType.MESH
HEUN = 0.25
F32 = jnp.float32
BF16 = jnp.bfloat16
I32 = jnp.int32
HOP, BACK = 11, 35
MOST = 8
LOGSTEP = 65536.0
TOP = 32767.0


def nn(left, right):
    return jnp.dot(left, right, preferred_element_type=F32)


def nt(left, right):
    return lax.dot_general(left, right, (((1,), (1,)), ((), ())), preferred_element_type=F32)


def tn(left, right):
    return lax.dot_general(left, right, (((0,), (0,)), ((), ())), preferred_element_type=F32)


def iota(shape, dim):
    return lax.broadcasted_iota(I32, shape, dim)


def split(value):
    high = value.astype(BF16)
    return high, (value - high.astype(F32)).astype(BF16)


def encode(value):
    peak = jnp.max(jnp.max(jnp.abs(value), axis=2, keepdims=True), axis=1, keepdims=True)
    level = jnp.ceil(jnp.log(jnp.maximum(peak, 1e-30)) * LOGSTEP).astype(I32)
    scale = TOP * jnp.exp(level.astype(F32) * (-1.0 / LOGSTEP))
    code = jnp.round(value * scale).astype(I32)
    return code, jnp.broadcast_to(level, (value.shape[0], 1, 128))


def pack(low, high):
    return jnp.bitwise_or(jnp.left_shift(high, 16), jnp.bitwise_and(low, 0xFFFF))


def unpack(word):
    low = jnp.right_shift(jnp.left_shift(word, 16), 16)
    return low.astype(F32), jnp.right_shift(word, 16).astype(F32)


def encode_wide(value):
    code, level = encode(value)
    word = pack(code[:, :, :256], code[:, :, 256:])
    return jnp.concatenate([word[:, :, :128], word[:, :, 128:]], axis=1), level


def unscale(level):
    return jnp.exp(level.astype(F32) * (1.0 / LOGSTEP)) * (1.0 / TOP)


def decode_wide(word, level):
    scale = unscale(level)
    low0, high0 = unpack(word[:, :8])
    low1, high1 = unpack(word[:, 8:])
    return jnp.concatenate([low0 * scale, low1 * scale, high0 * scale, high1 * scale], axis=2)


def encode_slice(value):
    codes, levels = zip(*(encode(value[:, :, 128 * b : 128 * (b + 1)]) for b in range(3)))
    lane = iota((value.shape[0], 1, 128), 2)
    level = jnp.where(lane == 0, levels[0], jnp.where(lane == 1, levels[1], levels[2]))
    return jnp.concatenate([pack(codes[0], codes[1]), pack(codes[2][:, :4], codes[2][:, 4:]), level], axis=1)


def decode_slice(word):
    scale = unscale(word[:, 12:13])
    low, high = unpack(word[:, :8])
    top, bottom = unpack(word[:, 8:12])
    last = jnp.concatenate([top, bottom], axis=1)
    return low * scale[:, :, 0:1], high * scale[:, :, 1:2], last * scale[:, :, 2:3]


def joined(blocks):
    return jnp.concatenate(blocks, axis=2)


def wanted_columns(table):
    shape = (1, MOST, 128)
    lane, sub = iota(shape, 2), iota(shape, 1)
    one = jnp.where((lane == sub) | (lane == sub + 2 * MOST), 1.0, 0.0)
    weight = jnp.where(lane == sub + MOST, 256.0, one)
    return jnp.sum(table * weight, axis=2, keepdims=True) - 1.0


def bytes_wait(ref, semaphore):
    pltpu.make_async_copy(ref, ref, semaphore).wait()


def main_kernel(
    devices,
    x_hbm, owner_ref, row_ref, noise_hbm, g_hbm, obs_hbm, w1_hbm, b1_ref, w2_hbm, b2_ref, c_hbm, inv_ref, sigma_ref,
    dprev_hbm, all_hbm,
    x_ref, noise_ref, g_ref, obs_ref, w1_ref, w2_ref, c_ref, dprev, inc_ref, arr_ref,
    wtab, wrow, send_rows, recv_rows, norm_src, norm_tab, ret, xx, aa, gf, gp, u0, u1, xnb, f0s, gxs, dots,
    acc1, acc2, accx, in1, in2, inx, sums, enc1, got1, half, enc2, got2, fin, whole,
    ssem, rsem, lsem, s1, r1, s2, r2, s3, r3, s4, r4, s5, r5, out_sem,
):
    me = lax.axis_index("particle")
    rows, width = x_ref.shape
    hidden = w1_ref.shape[1]
    chips = devices // 2
    core = lax.rem(me, 2)
    other = me + 1 - 2 * core
    stride = {"x": 2, "z": 8, "y": 32}
    coordinate = {axis: lax.rem(lax.div(me, by), 4) for axis, by in stride.items()}
    streams = (("x", "y", "z"), ("z", "x", "y"), ("y", "z", "x"))

    barrier = pltpu.get_barrier_semaphore()

    def greet(k, carry):
        pl.semaphore_signal(barrier, inc=1, device_id=(lax.rem(me + k, devices),), device_id_type=MESH)
        return carry

    lax.fori_loop(1, devices, greet, 0)
    loads = [
        pltpu.make_async_copy(source, target, lsem.at[i])
        for i, (source, target) in enumerate(
            (
                (x_hbm, x_ref),
                (w1_hbm, w1_ref),
                (w2_hbm, w2_ref),
                (noise_hbm, noise_ref),
                (g_hbm, g_ref),
                (obs_hbm, obs_ref),
                (c_hbm, c_ref),
            )
        )
    ]
    for load in loads:
        load.start()

    owner = owner_ref[...]
    row = row_ref[...]
    named = jnp.where(iota((devices, rows), 0) == owner, 1.0, 0.0)
    named_b = named.astype(BF16)
    earlier = jnp.where(iota((rows, rows), 0) < iota((rows, rows), 1), 1.0, 0.0).astype(BF16)
    slot = jnp.sum(nn(named_b, earlier) * named, axis=0, keepdims=True)
    part = iota((128, rows), 0)
    low = jnp.bitwise_and(row, 255).astype(F32)
    high = jnp.right_shift(row, 8).astype(F32)
    value = jnp.where(part < MOST, low, jnp.where(part < 2 * MOST, high, jnp.where(part < 3 * MOST, 1.0, 0.0)))
    value = jnp.where(jnp.bitwise_and(part, MOST - 1).astype(F32) == slot, value, 0.0)
    wrow[...] = nt(named_b, value.astype(BF16))

    def spread(d, carry):
        wtab[d] = wrow[pl.ds(d, 1), :]
        return carry

    lax.fori_loop(0, devices, spread, 0, unroll=8)
    eye = jnp.where(iota((rows, rows), 0) == iota((rows, rows), 1), 1.0, 0.0).astype(BF16)
    turn = jnp.bitwise_and((me - owner + devices) * BACK, devices - 1)
    pair = jnp.where(part == 0, turn.astype(F32), jnp.where(part == 1, slot, 0.0)).astype(BF16)
    turned = nt(eye, pair)
    place = turned[:, 0:1] * (2 * MOST) + turned[:, 1:2]
    flat = owner * MOST + slot.astype(I32)

    pl.semaphore_wait(barrier, devices - 1)

    def exchange(stage, source, target, per_partner, by_turn=False, low=1, high=devices):
        def send(k, carry):
            d = lax.rem(me + lax.rem(HOP * k, devices), devices)
            pltpu.make_async_remote_copy(
                src_ref=source.at[d] if per_partner else source.at[0],
                dst_ref=target.at[k] if by_turn else target.at[me],
                send_sem=ssem.at[stage],
                recv_sem=rsem.at[4 + lax.div(k, devices // 4)] if by_turn else rsem.at[stage],
                device_id=(d,),
                device_id_type=MESH,
            ).start()
            return carry

        lax.fori_loop(low, high, send, 0)

    def exchange_wait(stage, target):
        most = target.at[pl.ds(0, devices - 1)]
        bytes_wait(most, ssem.at[stage])
        bytes_wait(most, rsem.at[stage])

    exchange(0, wtab, inc_ref, True)
    inc_ref[me] = wtab[me]
    exchange_wait(0, inc_ref)

    group = 16

    def gather(i, carry):
        at = pl.multiple_of(i * group, group)
        column = wanted_columns(inc_ref[pl.ds(at, group)])
        onehot = jnp.where(column == iota((group, MOST, rows), 2).astype(F32), 1.0, 0.0)
        out = nn(onehot.reshape(group * MOST, rows).astype(BF16), x_ref[...])
        halves = jnp.concatenate(
            [out[:, : width // 2].reshape(group, MOST, width // 2), out[:, width // 2 :].reshape(group, MOST, width // 2)],
            axis=1,
        )
        send_rows[pl.ds(at, group)] = halves.astype(BF16)
        return carry

    loads[0].wait()
    lax.fori_loop(0, devices // group, gather, 0)
    exchange(1, send_rows, recv_rows, True, by_turn=True)
    recv_rows[0] = send_rows[me]
    for load in loads[1:]:
        load.wait()

    left = jnp.zeros((rows, width // 2), F32)
    right = left
    quarter = devices // 4
    for i in range(4):
        first = 1 if i == 0 else 0
        bytes_wait(recv_rows.at[pl.ds(0, quarter - first)], rsem.at[4 + i])
        block = recv_rows[i * quarter : (i + 1) * quarter].reshape(quarter * 2 * MOST, width // 2)
        index = (iota((rows, quarter * 2 * MOST), 1) + i * quarter * 2 * MOST).astype(F32)
        take_left = jnp.where(place == index, 1.0, 0.0).astype(BF16)
        take_right = jnp.where(place + MOST == index, 1.0, 0.0).astype(BF16)
        left = left + nn(take_left, block)
        right = right + nn(take_right, block)
    xx[rows:, : width // 2] = left.astype(BF16)
    xx[rows:, width // 2 :] = right.astype(BF16)
    bytes_wait(recv_rows.at[pl.ds(0, devices - 1)], ssem.at[1])

    x0 = xx[rows:, :]
    block = 256
    for n in range(0, hidden, block):
        t = jnp.tanh(nn(x0, w1_ref[:, n : n + block]) + b1_ref[:, n : n + block])
        aa[rows:, n : n + block] = t.astype(BF16)
        u0[:, n : n + block] = 1.0 - t * t
    for n in range(0, width, block):
        cols = slice(n, n + block)
        f = nn(aa[rows:, :], w2_ref[:, cols]) + b2_ref[:, cols]
        kick = sigma_ref[:, cols] * noise_ref[:, cols].astype(F32)
        f0s[:, cols] = f
        xx[:rows, cols] = (xx[rows:, cols].astype(F32) + HEUN * f + kick).astype(BF16)
    xp = xx[:rows, :]
    for n in range(0, hidden, block):
        t = jnp.tanh(nn(xp, w1_ref[:, n : n + block]) + b1_ref[:, n : n + block])
        aa[:rows, n : n + block] = t.astype(BF16)
        u1[:, n : n + block] = 1.0 - t * t
    for n in range(0, width, block):
        cols = slice(n, n + block)
        f = nn(aa[:rows, :], w2_ref[:, cols]) + b2_ref[:, cols]
        kick = sigma_ref[:, cols] * noise_ref[:, cols].astype(F32)
        xn = xx[rows:, cols].astype(F32) + 0.5 * HEUN * (f0s[:, cols] + f) + kick
        xnb[:, cols] = xn.astype(BF16)
    resid = (obs_ref[...].astype(F32) - nn(xnb[...], c_ref[...])) * inv_ref[...]
    loglik = -0.5 * jnp.sum(resid * resid, axis=1, keepdims=True)

    peak = jnp.max(loglik, axis=0, keepdims=True)
    total = jnp.sum(jnp.exp(loglik - peak), axis=0, keepdims=True)
    norm_src[0] = jnp.where(iota((1, 128), 1) == 0, peak, total)
    exchange(2, norm_src, norm_tab, False)
    norm_tab[me] = norm_src[0]
    exchange_wait(2, norm_tab)
    table = norm_tab[...]
    peaks, totals = table[:, :, 0:1], table[:, :, 1:2]
    top = jnp.max(peaks, axis=0, keepdims=True)
    mass = jnp.sum(totals * jnp.exp(peaks - top), axis=0, keepdims=True)
    weight = jnp.exp(loglik - top[0]) / mass[0] * float(rows * devices)

    dmean = (weight * resid * inv_ref[...]).astype(BF16)
    for n in range(0, width, block):
        cols = slice(n, n + block)
        gxn = g_ref[:, cols].astype(F32) + nt(dmean, c_ref[cols, :])
        gxs[:, cols] = gxn
        gf[:rows, cols] = (0.5 * HEUN * gxn).astype(BF16)
    for n in range(0, hidden, block):
        cols = slice(n, n + block)
        one = nt(gf[:rows, :], w2_ref[cols, :]) * u1[:, cols]
        gp[:rows, cols] = one.astype(BF16)
        dots[:, cols] = jnp.sum(one, axis=0, keepdims=True)
    for n in range(0, width, block):
        cols = slice(n, n + block)
        gxn = gxs[:, cols]
        gxp = nt(gp[:rows, :], w1_ref[cols, :])
        both = gxn + gxp
        gf0 = 0.5 * HEUN * gxn + HEUN * gxp
        gf[rows:, cols] = gf0.astype(BF16)
        gxs[:, cols] = both
        d_b2 = jnp.sum(0.5 * HEUN * gxn + gf0, axis=0, keepdims=True)
        d_sigma = jnp.sum(both * noise_ref[:, cols].astype(F32), axis=0, keepdims=True)
        for j in range(block // 128):
            at = n // 128 + j
            accx[1, 1, at : at + 1, :] = d_b2[:, 128 * j : 128 * (j + 1)]
            accx[1, 2, at : at + 1, :] = d_sigma[:, 128 * j : 128 * (j + 1)]
    def core_swap(i, source, target):
        swap = pltpu.make_async_remote_copy(
            src_ref=source, dst_ref=target, send_sem=ssem.at[8 + i], recv_sem=rsem.at[8 + i],
            device_id=(other,), device_id_type=MESH,
        )
        swap.start()
        return swap

    theirs = pl.ds((1 - core) * chips, chips)
    accx[0] = tn(xnb[...], dmean).reshape(chips, 8, 128)
    for n in range(0, hidden, block):
        acc2[n // 8 : (n + block) // 8] = tn(aa[:, n : n + block], gf[...]).reshape(block // 8, 8, width)

    swaps = [core_swap(0, acc2.at[theirs], in2)]
    for n in range(0, hidden, block):
        cols = slice(n, n + block)
        zero = nt(gf[rows:, :], w2_ref[cols, :]) * u0[:, cols]
        gp[rows:, cols] = zero.astype(BF16)
        d_b1 = dots[:, cols] + jnp.sum(zero, axis=0, keepdims=True)
        for j in range(block // 128):
            at = n // 128 + j
            accx[1, 0, at : at + 1, :] = d_b1[:, 128 * j : 128 * (j + 1)]
    accx[1, 1, 4:8, :] = jnp.zeros((4, 128), F32)
    accx[1, 2, 4:8, :] = jnp.zeros((4, 128), F32)
    accx[1, pl.ds(3, chips - 3)] = jnp.zeros((chips - 3, 8, 128), F32)
    swaps.append(core_swap(1, accx.at[1 - core], inx))
    for h in range(2):
        acc1[h * chips : (h + 1) * chips] = tn(xx[...], gp[:, h * width : (h + 1) * width]).reshape(chips, 8, width)
    swaps.append(core_swap(2, acc1.at[theirs], in1))
    for n in range(0, width, block):
        cols = slice(n, n + block)
        gxs[:, cols] = gxs[:, cols] + nt(gp[rows:, :], w1_ref[cols, :])


    gx_high, gx_low = split(gxs[...])

    def give(i, carry):
        at = pl.multiple_of(i * group, group)
        onehot = jnp.where(iota((group * MOST, rows), 0) + at * MOST == flat, 1.0, 0.0).astype(BF16)
        out = nn(onehot, gx_high) + nn(onehot, gx_low)
        word, level = encode_wide(out.reshape(group, MOST, width))
        ret[pl.ds(at, group)] = jnp.concatenate([word, level], axis=1)
        return carry

    lax.fori_loop(0, devices // group, give, 0)
    for swap in swaps:
        swap.wait()

    step = 4

    def prepare(i, carry):
        at = pl.multiple_of(i * step, step)
        mine = pl.ds(at, step)
        held = pl.ds(core * chips + at, step)
        one = in1[mine] + acc1[held]
        two = in2[mine] + acc2[held]
        rest = inx[mine] + accx[core, mine]
        values = (one[:, :, :384], two[:, :, :384], joined([one[:, :, 384:], two[:, :, 384:], rest]))
        for t in range(3):
            sums[t, mine] = values[t]
            enc1[t, mine] = encode_slice(values[t])
        return carry

    lax.fori_loop(0, chips // step, prepare, 0)

    plane = chips // 4
    along = []
    for k in (2, 1, 3):
        for t, (axis, _, _) in enumerate(streams):
            there = lax.rem(coordinate[axis] + k, 4)
            copy = pltpu.make_async_remote_copy(
                src_ref=enc1.at[t, pl.ds(there * plane, plane)], dst_ref=got1.at[t, k - 1],
                send_sem=s1.at[3 * t + k - 1], recv_sem=r1.at[3 * t + k - 1],
                device_id=(me + (there - coordinate[axis]) * stride[axis],), device_id_type=MESH,
            )
            copy.start()
            along.append((t, copy))

    part_one = devices * 5 // 8
    exchange(3, ret, arr_ref, True, high=part_one)
    arr_ref[me] = ret[me]

    home = [coordinate[axis] * plane for axis, _, _ in streams]
    spot = [coordinate[u] * 4 + coordinate[v] for _, u, v in streams]
    def over_plane(t, source, target, send_sem, recv_sem):
        axis, u, v = streams[t]
        base = core + coordinate[axis] * stride[axis]

        def send(k, carry):
            there = lax.rem(spot[t] + k, plane)
            d = base + lax.div(there, 4) * stride[u] + lax.rem(there, 4) * stride[v]
            pltpu.make_async_remote_copy(
                src_ref=source(there), dst_ref=target(k), send_sem=send_sem, recv_sem=recv_sem,
                device_id=(d,), device_id_type=MESH,
            ).start()
            return carry

        lax.fori_loop(1, plane, send, 0)

    for t in range(3):
        for stream, copy in along:
            if stream == t:
                copy.wait()

        def fold(i, carry):
            at = pl.multiple_of(i * step, step)
            value = sums[t, pl.ds(home[t] + at, step)]
            for k in range(3):
                value = value + joined(decode_slice(got1[t, k, pl.ds(at, step)]))
            half[t, pl.ds(at, step)] = value
            enc2[t, pl.ds(at, step)] = encode_slice(value)
            return carry

        lax.fori_loop(0, plane // step, fold, 0)
        over_plane(t, lambda there: enc2.at[t, there], lambda k: got2.at[t, k - 1], s2.at[t], r2.at[t])
    exchange(3, ret, arr_ref, True, low=part_one)
    for t in range(3):
        bytes_wait(got2.at[t], r2.at[t])
        value = half[t, spot[t]][None]
        for k in range(0, plane - 1, 5):
            value = value + jnp.sum(joined(decode_slice(got2[t, k : k + 5])), axis=0, keepdims=True)
        fin[t] = encode_slice(value)
        whole[t, home[t] + spot[t]] = fin[t, 0]
        over_plane(t, lambda there: fin.at[t, 0], lambda k: whole.at[t, home[t] + spot[t]], s3.at[t], r3.at[t])

    outs = []

    def publish(i, t, first):
        source = whole.at[t, pl.ds(first, plane)]
        target = all_hbm.at[core, t, pl.ds(first, plane)]
        keep = pltpu.make_async_copy(source, target, out_sem.at[i])
        give = pltpu.make_async_remote_copy(
            src_ref=source, dst_ref=target, send_sem=s5.at[i], recv_sem=r5.at[i],
            device_id=(other,), device_id_type=MESH,
        )
        keep.start()
        give.start()
        outs.append(keep)
        outs.append(give)

    along = []
    for t, (axis, _, _) in enumerate(streams):
        bytes_wait(got2.at[t], r3.at[t])
        for k in (2, 1, 3):
            there = lax.rem(coordinate[axis] + k, 4)
            held = whole.at[t, pl.ds(home[t], plane)]
            copy = pltpu.make_async_remote_copy(
                src_ref=held, dst_ref=held, send_sem=s4.at[3 * t + k - 1], recv_sem=r4.at[3 * t + k - 1],
                device_id=(me + (there - coordinate[axis]) * stride[axis],), device_id_type=MESH,
            )
            copy.start()
            along.append((t, k, copy))
        publish(t, t, home[t])
    exchange_wait(3, arr_ref)

    def settle(i, carry):
        at = pl.multiple_of(i * group, group)
        column = wanted_columns(inc_ref[pl.ds(at, group)])
        onehot = jnp.where(column == iota((group, MOST, rows), 2).astype(F32), 1.0, 0.0)
        onehot = onehot.reshape(group * MOST, rows).astype(BF16)
        word = arr_ref[pl.ds(at, group)]
        value = decode_wide(word[:, :16], word[:, 16:17]).reshape(group * MOST, width)
        upper, lower = split(value)
        return carry + tn(onehot, upper) + tn(onehot, lower)

    dprev[...] = lax.fori_loop(0, devices // group, settle, jnp.zeros((rows, width), F32))
    settled = pltpu.make_async_copy(dprev, dprev_hbm, lsem.at[7])
    settled.start()

    for t, k, copy in along:
        copy.wait_recv()
        first = lax.rem(coordinate[streams[t][0]] + 4 - k, 4) * plane
        publish(3 + 3 * t + k - 1, t, first)
    for t, k, copy in along:
        copy.wait_send()
    for t in range(3):
        bytes_wait(got2.at[t], s2.at[t])
        bytes_wait(got2.at[t], s3.at[t])
    for copy in outs:
        copy.wait()
    settled.wait()


def finish_kernel(dp_ref, all_ref, dprev_ref, dw1_ref, dw2_ref, dc_ref, db1_ref, db2_ref, dsigma_ref):
    i = pl.program_id(0)
    step = all_ref.shape[2]
    width = dprev_ref.shape[1]
    dprev_ref[...] = dp_ref[...]
    for core in range(2):
        first, second, third = (decode_slice(all_ref[core, t]) for t in range(3))
        for b in range(4):
            one = first[b] if b < 3 else third[0]
            two = second[b] if b < 3 else third[1]
            at = core * width + 128 * b
            dw1_ref[:, at : at + 128] = one.reshape(step * 8, 128)
            dw2_ref[core, :, 128 * b : 128 * (b + 1)] = two.reshape(step * 8, 128)
        rest = third[2]
        if core == 0:
            dc_ref[...] = rest.reshape(step * 8, 128)
        else:

            @pl.when(i == 0)
            def _():
                db1_ref[...] = rest[0]
                db2_ref[...] = rest[1, :4]
                dsigma_ref[...] = rest[2, :4]


def per_device(x_prev, anc_owner, anc_row, noise, g_new, obs, w1, b1, w2, b2, c_obs, inv_scale, sigma):
    devices = lax.axis_size("particle")
    chips = devices // 2
    plane = chips // 4
    rows, width = x_prev.shape
    hidden = w1.shape[1]
    vmem = pl.BlockSpec(memory_space=pltpu.VMEM)
    anywhere = pl.BlockSpec(memory_space=pl.ANY)
    dma = pltpu.SemaphoreType.DMA
    d_prev, sums = pl.pallas_call(
        functools.partial(main_kernel, devices),
        out_shape=(
            jax.ShapeDtypeStruct((rows, width), F32),
            jax.ShapeDtypeStruct((2, 3, chips, 13, 128), I32),
        ),
        in_specs=[anywhere, vmem, vmem, anywhere, anywhere, anywhere, anywhere, vmem, anywhere, vmem, anywhere, vmem, vmem],
        out_specs=(anywhere, anywhere),
        scratch_shapes=[
            pltpu.VMEM((rows, width), BF16),
            pltpu.VMEM((rows, width), BF16),
            pltpu.VMEM((rows, width), BF16),
            pltpu.VMEM((rows, 128), BF16),
            pltpu.VMEM((width, hidden), BF16),
            pltpu.VMEM((hidden, width), BF16),
            pltpu.VMEM((width, 128), BF16),
            pltpu.VMEM((rows, width), F32),
            pltpu.VMEM((devices, 1, 128), F32),
            pltpu.VMEM((devices, 17, 128), I32),
            pltpu.VMEM((devices, 1, 128), F32),
            pltpu.VMEM((devices, 128), F32),
            pltpu.VMEM((devices, 2 * MOST, width // 2), BF16),
            pltpu.VMEM((devices, 2 * MOST, width // 2), BF16),
            pltpu.VMEM((1, 1, 128), F32),
            pltpu.VMEM((devices, 1, 128), F32),
            pltpu.VMEM((devices, 17, 128), I32),
            pltpu.VMEM((2 * rows, width), BF16),
            pltpu.VMEM((2 * rows, hidden), BF16),
            pltpu.VMEM((2 * rows, width), BF16),
            pltpu.VMEM((2 * rows, hidden), BF16),
            pltpu.VMEM((rows, hidden), F32),
            pltpu.VMEM((rows, hidden), F32),
            pltpu.VMEM((rows, width), BF16),
            pltpu.VMEM((rows, width), F32),
            pltpu.VMEM((rows, width), F32),
            pltpu.VMEM((1, hidden), F32),
            pltpu.VMEM((devices, 8, width), F32),
            pltpu.VMEM((devices, 8, width), F32),
            pltpu.VMEM((2, chips, 8, 128), F32),
            pltpu.VMEM((chips, 8, width), F32),
            pltpu.VMEM((chips, 8, width), F32),
            pltpu.VMEM((chips, 8, 128), F32),
            pltpu.VMEM((3, chips, 8, 384), F32),
            pltpu.VMEM((3, chips, 13, 128), I32),
            pltpu.VMEM((3, 3, plane, 13, 128), I32),
            pltpu.VMEM((3, plane, 8, 384), F32),
            pltpu.VMEM((3, plane, 13, 128), I32),
            pltpu.VMEM((3, plane - 1, 13, 128), I32),
            pltpu.VMEM((3, 1, 13, 128), I32),
            pltpu.VMEM((3, chips, 13, 128), I32),
            dma((12,)), dma((12,)), dma((8,)),
            dma((9,)), dma((9,)), dma((3,)), dma((3,)), dma((3,)), dma((3,)), dma((9,)), dma((9,)),
            dma((12,)), dma((12,)), dma((12,)),
        ],
        compiler_params=pltpu.CompilerParams(collective_id=0, has_side_effects=True, vmem_limit_bytes=58 * 2**20),
        name="heun_step",
    )(
        x_prev, anc_owner.reshape(1, rows), anc_row.reshape(1, rows), noise, g_new, obs,
        w1, b1.reshape(1, hidden), w2, b2.reshape(1, width), c_obs, inv_scale.reshape(1, -1), sigma.reshape(1, width),
    )
    step = 32
    lines = step * 8
    d_prev, d_w1, d_w2, d_c, d_b1, d_b2, d_sigma = pl.pallas_call(
        finish_kernel,
        grid=(chips // step,),
        out_shape=(
            jax.ShapeDtypeStruct((rows, width), F32),
            jax.ShapeDtypeStruct((width, hidden), F32),
            jax.ShapeDtypeStruct((2, hidden // 2, width), F32),
            jax.ShapeDtypeStruct((width, 128), F32),
            jax.ShapeDtypeStruct((hidden // 128, 128), F32),
            jax.ShapeDtypeStruct((width // 128, 128), F32),
            jax.ShapeDtypeStruct((width // 128, 128), F32),
        ),
        in_specs=[
            pl.BlockSpec((lines, width), lambda i: (i, 0)),
            pl.BlockSpec((2, 3, step, 13, 128), lambda i: (0, 0, i, 0, 0)),
        ],
        out_specs=(
            pl.BlockSpec((lines, width), lambda i: (i, 0)),
            pl.BlockSpec((lines, hidden), lambda i: (i, 0)),
            pl.BlockSpec((2, lines, width), lambda i: (0, i, 0)),
            pl.BlockSpec((lines, 128), lambda i: (i, 0)),
            pl.BlockSpec((hidden // 128, 128), lambda i: (0, 0)),
            pl.BlockSpec((width // 128, 128), lambda i: (0, 0)),
            pl.BlockSpec((width // 128, 128), lambda i: (0, 0)),
        ),
        compiler_params=pltpu.CompilerParams(vmem_limit_bytes=58 * 2**20),
        name="place_results",
    )(d_prev, sums)
    return (
        d_prev, d_w1, d_b1.reshape(hidden), d_w2.reshape(hidden, width), d_b2.reshape(width), d_c, d_sigma.reshape(width),
    )


def solution(mesh):
    split_rows = P("particle", None)
    return jax.shard_map(
        per_device,
        mesh=mesh,
        in_specs=(split_rows, split_rows, P("particle"), split_rows, split_rows, split_rows) + (P(),) * 7,
        out_specs=(split_rows, P(), P(), P(), P(), P(), P()),
        check_vma=False,
    )
```

```python
import functools

import jax
import jax.numpy as jnp
from jax import lax
from jax.experimental import pallas as pl
from jax.experimental.pallas import tpu as pltpu
from jax.sharding import PartitionSpec as P

MESH = pl.DeviceIdType.MESH
HEUN = 0.25
F32 = jnp.float32
BF16 = jnp.bfloat16
I32 = jnp.int32
HOP, BACK = 11, 35
MOST = 8
LOGSTEP = 65536.0
TOP = 32767.0


def nn(left, right):
    return jnp.dot(left, right, preferred_element_type=F32)


def nt(left, right):
    return lax.dot_general(left, right, (((1,), (1,)), ((), ())), preferred_element_type=F32)


def tn(left, right):
    return lax.dot_general(left, right, (((0,), (0,)), ((), ())), preferred_element_type=F32)


def iota(shape, dim):
    return lax.broadcasted_iota(I32, shape, dim)


def split(value):
    high = value.astype(BF16)
    return high, (value - high.astype(F32)).astype(BF16)


def encode(value):
    peak = jnp.max(jnp.max(jnp.abs(value), axis=2, keepdims=True), axis=1, keepdims=True)
    level = jnp.ceil(jnp.log(jnp.maximum(peak, 1e-30)) * LOGSTEP).astype(I32)
    scale = TOP * jnp.exp(level.astype(F32) * (-1.0 / LOGSTEP))
    code = jnp.round(value * scale).astype(I32)
    return code, jnp.broadcast_to(level, (value.shape[0], 1, 128))


def pack(low, high):
    return jnp.bitwise_or(jnp.left_shift(high, 16), jnp.bitwise_and(low, 0xFFFF))


def unpack(word):
    low = jnp.right_shift(jnp.left_shift(word, 16), 16)
    return low.astype(F32), jnp.right_shift(word, 16).astype(F32)


def encode_wide(value):
    code, level = encode(value)
    word = pack(code[:, :, :256], code[:, :, 256:])
    return jnp.concatenate([word[:, :, :128], word[:, :, 128:]], axis=1), level


def unscale(level):
    return jnp.exp(level.astype(F32) * (1.0 / LOGSTEP)) * (1.0 / TOP)


def decode_wide(word, level):
    scale = unscale(level)
    low0, high0 = unpack(word[:, :8])
    low1, high1 = unpack(word[:, 8:])
    return jnp.concatenate([low0 * scale, low1 * scale, high0 * scale, high1 * scale], axis=2)


def encode_slice(value):
    codes, levels = zip(*(encode(value[:, :, 128 * b : 128 * (b + 1)]) for b in range(3)))
    lane = iota((value.shape[0], 1, 128), 2)
    level = jnp.where(lane == 0, levels[0], jnp.where(lane == 1, levels[1], levels[2]))
    return jnp.concatenate([pack(codes[0], codes[1]), pack(codes[2][:, :4], codes[2][:, 4:]), level], axis=1)


def decode_slice(word):
    scale = unscale(word[:, 12:13])
    low, high = unpack(word[:, :8])
    top, bottom = unpack(word[:, 8:12])
    last = jnp.concatenate([top, bottom], axis=1)
    return low * scale[:, :, 0:1], high * scale[:, :, 1:2], last * scale[:, :, 2:3]


def joined(blocks):
    return jnp.concatenate(blocks, axis=2)


def wanted_columns(table):
    shape = (1, MOST, 128)
    lane, sub = iota(shape, 2), iota(shape, 1)
    one = jnp.where((lane == sub) | (lane == sub + 2 * MOST), 1.0, 0.0)
    weight = jnp.where(lane == sub + MOST, 256.0, one)
    return jnp.sum(table * weight, axis=2, keepdims=True) - 1.0


def bytes_wait(ref, semaphore):
    pltpu.make_async_copy(ref, ref, semaphore).wait()


def main_kernel(
    devices,
    x_hbm, owner_ref, row_ref, noise_hbm, g_hbm, obs_hbm, w1_hbm, b1_ref, w2_hbm, b2_ref, c_hbm, inv_ref, sigma_ref,
    dprev_hbm, all_hbm,
    x_ref, noise_ref, g_ref, obs_ref, w1_ref, w2_ref, c_ref, dprev, inc_ref, arr_ref,
    wtab, wrow, send_rows, recv_rows, norm_src, norm_tab, ret, xx, aa, gf, gp, u0, u1, xnb, f0s, gxs, dots,
    acc1, acc2, accx, in1, in2, inx, sums, enc1, got1, half, enc2, got2, fin, whole,
    ssem, rsem, lsem, s1, r1, s2, r2, s3, r3, s4, r4, s5, r5, out_sem,
):
    me = lax.axis_index("particle")
    rows, width = x_ref.shape
    hidden = w1_ref.shape[1]
    chips = devices // 2
    core = lax.rem(me, 2)
    other = me + 1 - 2 * core
    stride = {"x": 2, "z": 8, "y": 32}
    coordinate = {axis: lax.rem(lax.div(me, by), 4) for axis, by in stride.items()}
    streams = (("x", "y", "z"), ("z", "x", "y"), ("y", "z", "x"))

    barrier = pltpu.get_barrier_semaphore()

    def greet(k, carry):
        pl.semaphore_signal(barrier, inc=1, device_id=(lax.rem(me + k, devices),), device_id_type=MESH)
        return carry

    lax.fori_loop(1, devices, greet, 0)
    loads = [
        pltpu.make_async_copy(source, target, lsem.at[i])
        for i, (source, target) in enumerate(
            (
                (x_hbm, x_ref),
                (w1_hbm, w1_ref),
                (w2_hbm, w2_ref),
                (noise_hbm, noise_ref),
                (g_hbm, g_ref),
                (obs_hbm, obs_ref),
                (c_hbm, c_ref),
            )
        )
    ]
    for load in loads:
        load.start()

    owner = owner_ref[...]
    row = row_ref[...]
    named = jnp.where(iota((devices, rows), 0) == owner, 1.0, 0.0)
    named_b = named.astype(BF16)
    earlier = jnp.where(iota((rows, rows), 0) < iota((rows, rows), 1), 1.0, 0.0).astype(BF16)
    slot = jnp.sum(nn(named_b, earlier) * named, axis=0, keepdims=True)
    part = iota((128, rows), 0)
    low = jnp.bitwise_and(row, 255).astype(F32)
    high = jnp.right_shift(row, 8).astype(F32)
    value = jnp.where(part < MOST, low, jnp.where(part < 2 * MOST, high, jnp.where(part < 3 * MOST, 1.0, 0.0)))
    value = jnp.where(jnp.bitwise_and(part, MOST - 1).astype(F32) == slot, value, 0.0)
    wrow[...] = nt(named_b, value.astype(BF16))

    def spread(d, carry):
        wtab[d] = wrow[pl.ds(d, 1), :]
        return carry

    lax.fori_loop(0, devices, spread, 0, unroll=8)
    eye = jnp.where(iota((rows, rows), 0) == iota((rows, rows), 1), 1.0, 0.0).astype(BF16)
    turn = jnp.bitwise_and((me - owner + devices) * BACK, devices - 1)
    pair = jnp.where(part == 0, turn.astype(F32), jnp.where(part == 1, slot, 0.0)).astype(BF16)
    turned = nt(eye, pair)
    place = turned[:, 0:1] * (2 * MOST) + turned[:, 1:2]
    flat = owner * MOST + slot.astype(I32)

    pl.semaphore_wait(barrier, devices - 1)

    def exchange(stage, source, target, per_partner, by_turn=False, low=1, high=devices):
        def send(k, carry):
            d = lax.rem(me + lax.rem(HOP * k, devices), devices)
            pltpu.make_async_remote_copy(
                src_ref=source.at[d] if per_partner else source.at[0],
                dst_ref=target.at[devices - k] if by_turn else target.at[me],
                send_sem=ssem.at[stage],
                recv_sem=rsem.at[stage],
                device_id=(d,),
                device_id_type=MESH,
            ).start()
            return carry

        lax.fori_loop(low, high, send, 0)

    def exchange_wait(stage, target):
        most = target.at[pl.ds(0, devices - 1)]
        bytes_wait(most, ssem.at[stage])
        bytes_wait(most, rsem.at[stage])

    exchange(0, wtab, inc_ref, True, by_turn=True)
    inc_ref[0] = wtab[me]
    exchange_wait(0, inc_ref)

    group = 16

    def gather(i, carry):
        at = i * group
        column = wanted_columns(inc_ref[pl.ds(at, group)])
        onehot = jnp.where(column == iota((group, MOST, rows), 2).astype(F32), 1.0, 0.0)
        out = nn(onehot.reshape(group * MOST, rows).astype(BF16), x_ref[...])
        halves = jnp.concatenate(
            [out[:, : width // 2].reshape(group, MOST, width // 2), out[:, width // 2 :].reshape(group, MOST, width // 2)],
            axis=1,
        )
        send_rows[pl.ds(at, group)] = halves.astype(BF16)
        return carry

    loads[0].wait()
    quarter = devices // 4

    def send_row(k, carry):
        pltpu.make_async_remote_copy(
            src_ref=send_rows.at[k],
            dst_ref=recv_rows.at[k],
            send_sem=ssem.at[1],
            recv_sem=rsem.at[4 + lax.div(k, quarter)],
            device_id=(lax.rem(me + lax.rem(HOP * k, devices), devices),),
            device_id_type=MESH,
        ).start()
        return carry

    for i in range(devices // group):
        gather(i, 0)
        lax.fori_loop(max(1, i * group), (i + 1) * group, send_row, 0)
    recv_rows[0] = send_rows[0]
    for load in loads[1:]:
        load.wait()

    left = jnp.zeros((rows, width // 2), F32)
    right = left
    for i in range(4):
        first = 1 if i == 0 else 0
        bytes_wait(recv_rows.at[pl.ds(0, quarter - first)], rsem.at[4 + i])
        block = recv_rows[i * quarter : (i + 1) * quarter].reshape(quarter * 2 * MOST, width // 2)
        index = (iota((rows, quarter * 2 * MOST), 1) + i * quarter * 2 * MOST).astype(F32)
        take_left = jnp.where(place == index, 1.0, 0.0).astype(BF16)
        take_right = jnp.where(place + MOST == index, 1.0, 0.0).astype(BF16)
        left = left + nn(take_left, block)
        right = right + nn(take_right, block)
    xx[rows:, : width // 2] = left.astype(BF16)
    xx[rows:, width // 2 :] = right.astype(BF16)
    bytes_wait(recv_rows.at[pl.ds(0, devices - 1)], ssem.at[1])

    x0 = xx[rows:, :]
    block = 256
    for n in range(0, hidden, block):
        t = jnp.tanh(nn(x0, w1_ref[:, n : n + block]) + b1_ref[:, n : n + block])
        aa[rows:, n : n + block] = t.astype(BF16)
        u0[:, n : n + block] = 1.0 - t * t
    for n in range(0, width, block):
        cols = slice(n, n + block)
        f = nn(aa[rows:, :], w2_ref[:, cols]) + b2_ref[:, cols]
        kick = sigma_ref[:, cols] * noise_ref[:, cols].astype(F32)
        f0s[:, cols] = f
        xx[:rows, cols] = (xx[rows:, cols].astype(F32) + HEUN * f + kick).astype(BF16)
    xp = xx[:rows, :]
    for n in range(0, hidden, block):
        t = jnp.tanh(nn(xp, w1_ref[:, n : n + block]) + b1_ref[:, n : n + block])
        aa[:rows, n : n + block] = t.astype(BF16)
        u1[:, n : n + block] = 1.0 - t * t
    for n in range(0, width, block):
        cols = slice(n, n + block)
        f = nn(aa[:rows, :], w2_ref[:, cols]) + b2_ref[:, cols]
        kick = sigma_ref[:, cols] * noise_ref[:, cols].astype(F32)
        xn = xx[rows:, cols].astype(F32) + 0.5 * HEUN * (f0s[:, cols] + f) + kick
        xnb[:, cols] = xn.astype(BF16)
    resid = (obs_ref[...].astype(F32) - nn(xnb[...], c_ref[...])) * inv_ref[...]
    loglik = -0.5 * jnp.sum(resid * resid, axis=1, keepdims=True)

    peak = jnp.max(loglik, axis=0, keepdims=True)
    total = jnp.sum(jnp.exp(loglik - peak), axis=0, keepdims=True)
    norm_src[0] = jnp.where(iota((1, 128), 1) == 0, peak, total)
    exchange(2, norm_src, norm_tab, False)
    norm_tab[me] = norm_src[0]
    exchange_wait(2, norm_tab)
    table = norm_tab[...]
    peaks, totals = table[:, :, 0:1], table[:, :, 1:2]
    top = jnp.max(peaks, axis=0, keepdims=True)
    mass = jnp.sum(totals * jnp.exp(peaks - top), axis=0, keepdims=True)
    weight = jnp.exp(loglik - top[0]) / mass[0] * float(rows * devices)

    dmean = (weight * resid * inv_ref[...]).astype(BF16)
    for n in range(0, width, block):
        cols = slice(n, n + block)
        gxn = g_ref[:, cols].astype(F32) + nt(dmean, c_ref[cols, :])
        gxs[:, cols] = gxn
        gf[:rows, cols] = (0.5 * HEUN * gxn).astype(BF16)
    for n in range(0, hidden, block):
        cols = slice(n, n + block)
        one = nt(gf[:rows, :], w2_ref[cols, :]) * u1[:, cols]
        gp[:rows, cols] = one.astype(BF16)
        dots[:, cols] = jnp.sum(one, axis=0, keepdims=True)
    for n in range(0, width, block):
        cols = slice(n, n + block)
        gxn = gxs[:, cols]
        gxp = nt(gp[:rows, :], w1_ref[cols, :])
        both = gxn + gxp
        gf0 = 0.5 * HEUN * gxn + HEUN * gxp
        gf[rows:, cols] = gf0.astype(BF16)
        gxs[:, cols] = both
        d_b2 = jnp.sum(0.5 * HEUN * gxn + gf0, axis=0, keepdims=True)
        d_sigma = jnp.sum(both * noise_ref[:, cols].astype(F32), axis=0, keepdims=True)
        for j in range(block // 128):
            at = n // 128 + j
            accx[1, 1, at : at + 1, :] = d_b2[:, 128 * j : 128 * (j + 1)]
            accx[1, 2, at : at + 1, :] = d_sigma[:, 128 * j : 128 * (j + 1)]
    def core_swap(i, source, target):
        swap = pltpu.make_async_remote_copy(
            src_ref=source, dst_ref=target, send_sem=ssem.at[8 + i], recv_sem=rsem.at[8 + i],
            device_id=(other,), device_id_type=MESH,
        )
        swap.start()
        return swap

    theirs = pl.ds((1 - core) * chips, chips)
    accx[0] = tn(xnb[...], dmean).reshape(chips, 8, 128)
    for n in range(0, hidden, block):
        acc2[n // 8 : (n + block) // 8] = tn(aa[:, n : n + block], gf[...]).reshape(block // 8, 8, width)

    swaps = [core_swap(0, acc2.at[theirs], in2)]
    for n in range(0, hidden, block):
        cols = slice(n, n + block)
        zero = nt(gf[rows:, :], w2_ref[cols, :]) * u0[:, cols]
        gp[rows:, cols] = zero.astype(BF16)
        d_b1 = dots[:, cols] + jnp.sum(zero, axis=0, keepdims=True)
        for j in range(block // 128):
            at = n // 128 + j
            accx[1, 0, at : at + 1, :] = d_b1[:, 128 * j : 128 * (j + 1)]
    accx[1, 1, 4:8, :] = jnp.zeros((4, 128), F32)
    accx[1, 2, 4:8, :] = jnp.zeros((4, 128), F32)
    accx[1, pl.ds(3, chips - 3)] = jnp.zeros((chips - 3, 8, 128), F32)
    swaps.append(core_swap(1, accx.at[1 - core], inx))
    for h in range(2):
        acc1[h * chips : (h + 1) * chips] = tn(xx[...], gp[:, h * width : (h + 1) * width]).reshape(chips, 8, width)
    swaps.append(core_swap(2, acc1.at[theirs], in1))
    for n in range(0, width, block):
        cols = slice(n, n + block)
        gxs[:, cols] = gxs[:, cols] + nt(gp[rows:, :], w1_ref[cols, :])


    gx_high, gx_low = split(gxs[...])

    def give(i, carry):
        at = pl.multiple_of(i * group, group)
        onehot = jnp.where(iota((group * MOST, rows), 0) + at * MOST == flat, 1.0, 0.0).astype(BF16)
        out = nn(onehot, gx_high) + nn(onehot, gx_low)
        word, level = encode_wide(out.reshape(group, MOST, width))
        ret[pl.ds(at, group)] = jnp.concatenate([word, level], axis=1)
        return carry

    lax.fori_loop(0, devices // group, give, 0)
    for swap in swaps:
        swap.wait()

    step = 4

    def prepare(i, carry):
        at = pl.multiple_of(i * step, step)
        mine = pl.ds(at, step)
        held = pl.ds(core * chips + at, step)
        one = in1[mine] + acc1[held]
        two = in2[mine] + acc2[held]
        rest = inx[mine] + accx[core, mine]
        values = (one[:, :, :384], two[:, :, :384], joined([one[:, :, 384:], two[:, :, 384:], rest]))
        for t in range(3):
            sums[t, mine] = values[t]
            enc1[t, mine] = encode_slice(values[t])
        return carry

    lax.fori_loop(0, chips // step, prepare, 0)

    plane = chips // 4
    along = []
    for k in (2, 1, 3):
        for t, (axis, _, _) in enumerate(streams):
            there = lax.rem(coordinate[axis] + k, 4)
            copy = pltpu.make_async_remote_copy(
                src_ref=enc1.at[t, pl.ds(there * plane, plane)], dst_ref=got1.at[t, k - 1],
                send_sem=s1.at[3 * t + k - 1], recv_sem=r1.at[3 * t + k - 1],
                device_id=(me + (there - coordinate[axis]) * stride[axis],), device_id_type=MESH,
            )
            copy.start()
            along.append((t, copy))

    part_one = devices * 5 // 8
    exchange(3, ret, arr_ref, True, by_turn=True, high=part_one)
    arr_ref[0] = ret[me]

    home = [coordinate[axis] * plane for axis, _, _ in streams]
    spot = [coordinate[u] * 4 + coordinate[v] for _, u, v in streams]
    def over_plane(t, source, target, send_sem, recv_sem):
        axis, u, v = streams[t]
        base = core + coordinate[axis] * stride[axis]

        def send(k, carry):
            there = lax.rem(spot[t] + k, plane)
            d = base + lax.div(there, 4) * stride[u] + lax.rem(there, 4) * stride[v]
            pltpu.make_async_remote_copy(
                src_ref=source(there), dst_ref=target(k), send_sem=send_sem, recv_sem=recv_sem,
                device_id=(d,), device_id_type=MESH,
            ).start()
            return carry

        lax.fori_loop(1, plane, send, 0)

    for t in range(3):
        for stream, copy in along:
            if stream == t:
                copy.wait()

        def fold(i, carry):
            at = pl.multiple_of(i * step, step)
            value = sums[t, pl.ds(home[t] + at, step)]
            for k in range(3):
                value = value + joined(decode_slice(got1[t, k, pl.ds(at, step)]))
            half[t, pl.ds(at, step)] = value
            enc2[t, pl.ds(at, step)] = encode_slice(value)
            return carry

        lax.fori_loop(0, plane // step, fold, 0)
        over_plane(t, lambda there: enc2.at[t, there], lambda k: got2.at[t, k - 1], s2.at[t], r2.at[t])
    exchange(3, ret, arr_ref, True, by_turn=True, low=part_one)
    for t in range(3):
        bytes_wait(got2.at[t], r2.at[t])
        value = half[t, spot[t]][None]
        for k in range(0, plane - 1, 5):
            value = value + jnp.sum(joined(decode_slice(got2[t, k : k + 5])), axis=0, keepdims=True)
        fin[t] = encode_slice(value)
        whole[t, home[t] + spot[t]] = fin[t, 0]
        over_plane(t, lambda there: fin.at[t, 0], lambda k: whole.at[t, home[t] + spot[t]], s3.at[t], r3.at[t])

    outs = []

    def publish(i, t, first):
        source = whole.at[t, pl.ds(first, plane)]
        target = all_hbm.at[core, t, pl.ds(first, plane)]
        keep = pltpu.make_async_copy(source, target, out_sem.at[i])
        give = pltpu.make_async_remote_copy(
            src_ref=source, dst_ref=target, send_sem=s5.at[i], recv_sem=r5.at[i],
            device_id=(other,), device_id_type=MESH,
        )
        keep.start()
        give.start()
        outs.append(keep)
        outs.append(give)

    along = []
    for t, (axis, _, _) in enumerate(streams):
        bytes_wait(got2.at[t], r3.at[t])
        for k in (2, 1, 3):
            there = lax.rem(coordinate[axis] + k, 4)
            held = whole.at[t, pl.ds(home[t], plane)]
            copy = pltpu.make_async_remote_copy(
                src_ref=held, dst_ref=held, send_sem=s4.at[3 * t + k - 1], recv_sem=r4.at[3 * t + k - 1],
                device_id=(me + (there - coordinate[axis]) * stride[axis],), device_id_type=MESH,
            )
            copy.start()
            along.append((t, k, copy))
        publish(t, t, home[t])
    exchange_wait(3, arr_ref)

    def settle(i, carry):
        at = pl.multiple_of(i * group, group)
        column = wanted_columns(inc_ref[pl.ds(at, group)])
        onehot = jnp.where(column == iota((group, MOST, rows), 2).astype(F32), 1.0, 0.0)
        onehot = onehot.reshape(group * MOST, rows).astype(BF16)
        word = arr_ref[pl.ds(at, group)]
        value = decode_wide(word[:, :16], word[:, 16:17]).reshape(group * MOST, width)
        upper, lower = split(value)
        return carry + tn(onehot, upper) + tn(onehot, lower)

    dprev[...] = lax.fori_loop(0, devices // group, settle, jnp.zeros((rows, width), F32))
    settled = pltpu.make_async_copy(dprev, dprev_hbm, lsem.at[7])
    settled.start()

    for t, k, copy in along:
        copy.wait_recv()
        first = lax.rem(coordinate[streams[t][0]] + 4 - k, 4) * plane
        publish(3 + 3 * t + k - 1, t, first)
    for t, k, copy in along:
        copy.wait_send()
    for t in range(3):
        bytes_wait(got2.at[t], s2.at[t])
        bytes_wait(got2.at[t], s3.at[t])
    for copy in outs:
        copy.wait()
    settled.wait()


def finish_kernel(dp_ref, all_ref, dprev_ref, dw1_ref, dw2_ref, dc_ref, db1_ref, db2_ref, dsigma_ref):
    i = pl.program_id(0)
    step = all_ref.shape[2]
    width = dprev_ref.shape[1]
    dprev_ref[...] = dp_ref[...]
    for core in range(2):
        first, second, third = (decode_slice(all_ref[core, t]) for t in range(3))
        for b in range(4):
            one = first[b] if b < 3 else third[0]
            two = second[b] if b < 3 else third[1]
            at = core * width + 128 * b
            dw1_ref[:, at : at + 128] = one.reshape(step * 8, 128)
            dw2_ref[core, :, 128 * b : 128 * (b + 1)] = two.reshape(step * 8, 128)
        rest = third[2]
        if core == 0:
            dc_ref[...] = rest.reshape(step * 8, 128)
        else:

            @pl.when(i == 0)
            def _():
                db1_ref[...] = rest[0]
                db2_ref[...] = rest[1, :4]
                dsigma_ref[...] = rest[2, :4]


def per_device(x_prev, anc_owner, anc_row, noise, g_new, obs, w1, b1, w2, b2, c_obs, inv_scale, sigma):
    devices = lax.axis_size("particle")
    chips = devices // 2
    plane = chips // 4
    rows, width = x_prev.shape
    hidden = w1.shape[1]
    vmem = pl.BlockSpec(memory_space=pltpu.VMEM)
    anywhere = pl.BlockSpec(memory_space=pl.ANY)
    dma = pltpu.SemaphoreType.DMA
    d_prev, sums = pl.pallas_call(
        functools.partial(main_kernel, devices),
        out_shape=(
            jax.ShapeDtypeStruct((rows, width), F32),
            jax.ShapeDtypeStruct((2, 3, chips, 13, 128), I32),
        ),
        in_specs=[anywhere, vmem, vmem, anywhere, anywhere, anywhere, anywhere, vmem, anywhere, vmem, anywhere, vmem, vmem],
        out_specs=(anywhere, anywhere),
        scratch_shapes=[
            pltpu.VMEM((rows, width), BF16),
            pltpu.VMEM((rows, width), BF16),
            pltpu.VMEM((rows, width), BF16),
            pltpu.VMEM((rows, 128), BF16),
            pltpu.VMEM((width, hidden), BF16),
            pltpu.VMEM((hidden, width), BF16),
            pltpu.VMEM((width, 128), BF16),
            pltpu.VMEM((rows, width), F32),
            pltpu.VMEM((devices, 1, 128), F32),
            pltpu.VMEM((devices, 17, 128), I32),
            pltpu.VMEM((devices, 1, 128), F32),
            pltpu.VMEM((devices, 128), F32),
            pltpu.VMEM((devices, 2 * MOST, width // 2), BF16),
            pltpu.VMEM((devices, 2 * MOST, width // 2), BF16),
            pltpu.VMEM((1, 1, 128), F32),
            pltpu.VMEM((devices, 1, 128), F32),
            pltpu.VMEM((devices, 17, 128), I32),
            pltpu.VMEM((2 * rows, width), BF16),
            pltpu.VMEM((2 * rows, hidden), BF16),
            pltpu.VMEM((2 * rows, width), BF16),
            pltpu.VMEM((2 * rows, hidden), BF16),
            pltpu.VMEM((rows, hidden), F32),
            pltpu.VMEM((rows, hidden), F32),
            pltpu.VMEM((rows, width), BF16),
            pltpu.VMEM((rows, width), F32),
            pltpu.VMEM((rows, width), F32),
            pltpu.VMEM((1, hidden), F32),
            pltpu.VMEM((devices, 8, width), F32),
            pltpu.VMEM((devices, 8, width), F32),
            pltpu.VMEM((2, chips, 8, 128), F32),
            pltpu.VMEM((chips, 8, width), F32),
            pltpu.VMEM((chips, 8, width), F32),
            pltpu.VMEM((chips, 8, 128), F32),
            pltpu.VMEM((3, chips, 8, 384), F32),
            pltpu.VMEM((3, chips, 13, 128), I32),
            pltpu.VMEM((3, 3, plane, 13, 128), I32),
            pltpu.VMEM((3, plane, 8, 384), F32),
            pltpu.VMEM((3, plane, 13, 128), I32),
            pltpu.VMEM((3, plane - 1, 13, 128), I32),
            pltpu.VMEM((3, 1, 13, 128), I32),
            pltpu.VMEM((3, chips, 13, 128), I32),
            dma((12,)), dma((12,)), dma((8,)),
            dma((9,)), dma((9,)), dma((3,)), dma((3,)), dma((3,)), dma((3,)), dma((9,)), dma((9,)),
            dma((12,)), dma((12,)), dma((12,)),
        ],
        compiler_params=pltpu.CompilerParams(collective_id=0, has_side_effects=True, vmem_limit_bytes=58 * 2**20),
        name="heun_step",
    )(
        x_prev, anc_owner.reshape(1, rows), anc_row.reshape(1, rows), noise, g_new, obs,
        w1, b1.reshape(1, hidden), w2, b2.reshape(1, width), c_obs, inv_scale.reshape(1, -1), sigma.reshape(1, width),
    )
    step = 32
    lines = step * 8
    d_prev, d_w1, d_w2, d_c, d_b1, d_b2, d_sigma = pl.pallas_call(
        finish_kernel,
        grid=(chips // step,),
        out_shape=(
            jax.ShapeDtypeStruct((rows, width), F32),
            jax.ShapeDtypeStruct((width, hidden), F32),
            jax.ShapeDtypeStruct((2, hidden // 2, width), F32),
            jax.ShapeDtypeStruct((width, 128), F32),
            jax.ShapeDtypeStruct((hidden // 128, 128), F32),
            jax.ShapeDtypeStruct((width // 128, 128), F32),
            jax.ShapeDtypeStruct((width // 128, 128), F32),
        ),
        in_specs=[
            pl.BlockSpec((lines, width), lambda i: (i, 0)),
            pl.BlockSpec((2, 3, step, 13, 128), lambda i: (0, 0, i, 0, 0)),
        ],
        out_specs=(
            pl.BlockSpec((lines, width), lambda i: (i, 0)),
            pl.BlockSpec((lines, hidden), lambda i: (i, 0)),
            pl.BlockSpec((2, lines, width), lambda i: (0, i, 0)),
            pl.BlockSpec((lines, 128), lambda i: (i, 0)),
            pl.BlockSpec((hidden // 128, 128), lambda i: (0, 0)),
            pl.BlockSpec((width // 128, 128), lambda i: (0, 0)),
            pl.BlockSpec((width // 128, 128), lambda i: (0, 0)),
        ),
        compiler_params=pltpu.CompilerParams(vmem_limit_bytes=58 * 2**20),
        name="place_results",
    )(d_prev, sums)
    return (
        d_prev, d_w1, d_b1.reshape(hidden), d_w2.reshape(hidden, width), d_b2.reshape(width), d_c, d_sigma.reshape(width),
    )


def solution(mesh):
    split_rows = P("particle", None)
    return jax.shard_map(
        per_device,
        mesh=mesh,
        in_specs=(split_rows, split_rows, P("particle"), split_rows, split_rows, split_rows) + (P(),) * 7,
        out_specs=(split_rows, P(), P(), P(), P(), P(), P()),
        check_vma=False,
    )
```

```python
import functools

import jax
import jax.numpy as jnp
from jax import lax
from jax.experimental import pallas as pl
from jax.experimental.pallas import tpu as pltpu
from jax.sharding import PartitionSpec as P

MESH = pl.DeviceIdType.MESH
HEUN = 0.25
F32 = jnp.float32
BF16 = jnp.bfloat16
I32 = jnp.int32
HOP, BACK = 11, 35
MOST = 8
LOGSTEP = 65536.0
TOP = 32767.0


def nn(left, right):
    return jnp.dot(left, right, preferred_element_type=F32)


def nt(left, right):
    return lax.dot_general(left, right, (((1,), (1,)), ((), ())), preferred_element_type=F32)


def tn(left, right):
    return lax.dot_general(left, right, (((0,), (0,)), ((), ())), preferred_element_type=F32)


def iota(shape, dim):
    return lax.broadcasted_iota(I32, shape, dim)


def split(value):
    high = value.astype(BF16)
    return high, (value - high.astype(F32)).astype(BF16)


def encode(value):
    peak = jnp.max(jnp.max(jnp.abs(value), axis=2, keepdims=True), axis=1, keepdims=True)
    level = jnp.ceil(jnp.log(jnp.maximum(peak, 1e-30)) * LOGSTEP).astype(I32)
    scale = TOP * jnp.exp(level.astype(F32) * (-1.0 / LOGSTEP))
    code = jnp.round(value * scale).astype(I32)
    return code, jnp.broadcast_to(level, (value.shape[0], 1, 128))


def pack(low, high):
    return jnp.bitwise_or(jnp.left_shift(high, 16), jnp.bitwise_and(low, 0xFFFF))


def unpack(word):
    low = jnp.right_shift(jnp.left_shift(word, 16), 16)
    return low.astype(F32), jnp.right_shift(word, 16).astype(F32)


def encode_wide(value):
    code, level = encode(value)
    word = pack(code[:, :, :256], code[:, :, 256:])
    return jnp.concatenate([word[:, :, :128], word[:, :, 128:]], axis=1), level


def unscale(level):
    return jnp.exp(level.astype(F32) * (1.0 / LOGSTEP)) * (1.0 / TOP)


def decode_wide(word, level):
    scale = unscale(level)
    low0, high0 = unpack(word[:, :8])
    low1, high1 = unpack(word[:, 8:])
    return jnp.concatenate([low0 * scale, low1 * scale, high0 * scale, high1 * scale], axis=2)


def encode_slice(value):
    codes, levels = zip(*(encode(value[:, :, 128 * b : 128 * (b + 1)]) for b in range(3)))
    lane = iota((value.shape[0], 1, 128), 2)
    level = jnp.where(lane == 0, levels[0], jnp.where(lane == 1, levels[1], levels[2]))
    return jnp.concatenate([pack(codes[0], codes[1]), pack(codes[2][:, :4], codes[2][:, 4:]), level], axis=1)


def decode_slice(word):
    scale = unscale(word[:, 12:13])
    low, high = unpack(word[:, :8])
    top, bottom = unpack(word[:, 8:12])
    last = jnp.concatenate([top, bottom], axis=1)
    return low * scale[:, :, 0:1], high * scale[:, :, 1:2], last * scale[:, :, 2:3]


def joined(blocks):
    return jnp.concatenate(blocks, axis=2)


def wanted_columns(table):
    shape = (1, MOST, 128)
    lane, sub = iota(shape, 2), iota(shape, 1)
    one = jnp.where((lane == sub) | (lane == sub + 2 * MOST), 1.0, 0.0)
    weight = jnp.where(lane == sub + MOST, 256.0, one)
    return jnp.sum(table * weight, axis=2, keepdims=True) - 1.0


def bytes_wait(ref, semaphore):
    pltpu.make_async_copy(ref, ref, semaphore).wait()


def main_kernel(
    devices,
    x_hbm, owner_ref, row_ref, noise_hbm, g_hbm, obs_hbm, w1_hbm, b1_ref, w2_hbm, b2_ref, c_hbm, inv_ref, sigma_ref,
    dprev_hbm, all_hbm,
    x_ref, noise_ref, g_ref, obs_ref, w1_ref, w2_ref, c_ref, dprev, inc_ref, arr_ref,
    wtab, wrow, send_rows, recv_rows, norm_src, norm_tab, ret, xx, aa, gf, gp, u0, u1, xnb, f0s, gxs, dots,
    acc1, acc2, accx, in1, in2, inx, sums, enc1, got1, half, enc2, got2, fin, whole,
    ssem, rsem, lsem, s1, r1, s2, r2, s3, r3, s4, r4, s5, r5, out_sem,
):
    me = lax.axis_index("particle")
    rows, width = x_ref.shape
    hidden = w1_ref.shape[1]
    chips = devices // 2
    core = lax.rem(me, 2)
    other = me + 1 - 2 * core
    stride = {"x": 2, "z": 8, "y": 32}
    coordinate = {axis: lax.rem(lax.div(me, by), 4) for axis, by in stride.items()}
    streams = (("x", "y", "z"), ("z", "x", "y"), ("y", "z", "x"))

    barrier = pltpu.get_barrier_semaphore()

    def greet(k, carry):
        pl.semaphore_signal(barrier, inc=1, device_id=(lax.rem(me + k, devices),), device_id_type=MESH)
        return carry

    lax.fori_loop(1, devices, greet, 0)
    loads = [
        pltpu.make_async_copy(source, target, lsem.at[i])
        for i, (source, target) in enumerate(
            (
                (x_hbm, x_ref),
                (w1_hbm, w1_ref),
                (w2_hbm, w2_ref),
                (noise_hbm, noise_ref),
                (g_hbm, g_ref),
                (obs_hbm, obs_ref),
                (c_hbm, c_ref),
            )
        )
    ]
    for load in loads:
        load.start()

    owner = owner_ref[...]
    row = row_ref[...]
    named = jnp.where(iota((devices, rows), 0) == owner, 1.0, 0.0)
    named_b = named.astype(BF16)
    earlier = jnp.where(iota((rows, rows), 0) < iota((rows, rows), 1), 1.0, 0.0).astype(BF16)
    slot = jnp.sum(nn(named_b, earlier) * named, axis=0, keepdims=True)
    part = iota((128, rows), 0)
    low = jnp.bitwise_and(row, 255).astype(F32)
    high = jnp.right_shift(row, 8).astype(F32)
    value = jnp.where(part < MOST, low, jnp.where(part < 2 * MOST, high, jnp.where(part < 3 * MOST, 1.0, 0.0)))
    value = jnp.where(jnp.bitwise_and(part, MOST - 1).astype(F32) == slot, value, 0.0)
    wrow[...] = nt(named_b, value.astype(BF16))

    def spread(d, carry):
        wtab[d] = wrow[pl.ds(d, 1), :]
        return carry

    lax.fori_loop(0, devices, spread, 0, unroll=8)
    eye = jnp.where(iota((rows, rows), 0) == iota((rows, rows), 1), 1.0, 0.0).astype(BF16)
    turn = jnp.bitwise_and((me - owner + devices) * BACK, devices - 1)
    pair = jnp.where(part == 0, turn.astype(F32), jnp.where(part == 1, slot, 0.0)).astype(BF16)
    turned = nt(eye, pair)
    place = turned[:, 0:1] * (2 * MOST) + turned[:, 1:2]
    flat = owner * MOST + slot.astype(I32)

    pl.semaphore_wait(barrier, devices - 1)

    def exchange(stage, source, target, per_partner, by_turn=False, low=1, high=devices):
        def send(k, carry):
            d = lax.rem(me + lax.rem(HOP * k, devices), devices)
            pltpu.make_async_remote_copy(
                src_ref=source.at[d] if per_partner else source.at[0],
                dst_ref=target.at[devices - k] if by_turn else target.at[me],
                send_sem=ssem.at[stage],
                recv_sem=rsem.at[stage],
                device_id=(d,),
                device_id_type=MESH,
            ).start()
            return carry

        lax.fori_loop(low, high, send, 0)

    def exchange_wait(stage, target):
        most = target.at[pl.ds(0, devices - 1)]
        bytes_wait(most, ssem.at[stage])
        bytes_wait(most, rsem.at[stage])

    exchange(0, wtab, inc_ref, True, by_turn=True)
    inc_ref[0] = wtab[me]
    exchange_wait(0, inc_ref)

    group = 16

    def gather(i, carry):
        at = i * group
        column = wanted_columns(inc_ref[pl.ds(at, group)])
        onehot = jnp.where(column == iota((group, MOST, rows), 2).astype(F32), 1.0, 0.0)
        out = nn(onehot.reshape(group * MOST, rows).astype(BF16), x_ref[...])
        halves = jnp.concatenate(
            [out[:, : width // 2].reshape(group, MOST, width // 2), out[:, width // 2 :].reshape(group, MOST, width // 2)],
            axis=1,
        )
        send_rows[pl.ds(at, group)] = halves.astype(BF16)
        return carry

    loads[0].wait()
    share = devices // 8

    def send_row(k, carry):
        pltpu.make_async_remote_copy(
            src_ref=send_rows.at[k],
            dst_ref=recv_rows.at[k],
            send_sem=ssem.at[1],
            recv_sem=rsem.at[4 + lax.div(k, share)],
            device_id=(lax.rem(me + lax.rem(HOP * k, devices), devices),),
            device_id_type=MESH,
        ).start()
        return carry

    for i in range(devices // group):
        gather(i, 0)
        lax.fori_loop(max(1, i * group), (i + 1) * group, send_row, 0)
    recv_rows[0] = send_rows[0]
    for load in loads[1:]:
        load.wait()

    left = jnp.zeros((rows, width // 2), F32)
    right = left
    for i in range(8):
        first = 1 if i == 0 else 0
        bytes_wait(recv_rows.at[pl.ds(0, share - first)], rsem.at[4 + i])
        block = recv_rows[i * share : (i + 1) * share].reshape(share * 2 * MOST, width // 2)
        index = (iota((rows, share * 2 * MOST), 1) + i * share * 2 * MOST).astype(F32)
        take_left = jnp.where(place == index, 1.0, 0.0).astype(BF16)
        take_right = jnp.where(place + MOST == index, 1.0, 0.0).astype(BF16)
        left = left + nn(take_left, block)
        right = right + nn(take_right, block)
    xx[rows:, : width // 2] = left.astype(BF16)
    xx[rows:, width // 2 :] = right.astype(BF16)
    bytes_wait(recv_rows.at[pl.ds(0, devices - 1)], ssem.at[1])

    x0 = xx[rows:, :]
    block = 256
    for n in range(0, hidden, block):
        t = jnp.tanh(nn(x0, w1_ref[:, n : n + block]) + b1_ref[:, n : n + block])
        aa[rows:, n : n + block] = t.astype(BF16)
        u0[:, n : n + block] = 1.0 - t * t
    for n in range(0, width, block):
        cols = slice(n, n + block)
        f = nn(aa[rows:, :], w2_ref[:, cols]) + b2_ref[:, cols]
        kick = sigma_ref[:, cols] * noise_ref[:, cols].astype(F32)
        f0s[:, cols] = f
        xx[:rows, cols] = (xx[rows:, cols].astype(F32) + HEUN * f + kick).astype(BF16)
    xp = xx[:rows, :]
    for n in range(0, hidden, block):
        t = jnp.tanh(nn(xp, w1_ref[:, n : n + block]) + b1_ref[:, n : n + block])
        aa[:rows, n : n + block] = t.astype(BF16)
        u1[:, n : n + block] = 1.0 - t * t
    for n in range(0, width, block):
        cols = slice(n, n + block)
        f = nn(aa[:rows, :], w2_ref[:, cols]) + b2_ref[:, cols]
        kick = sigma_ref[:, cols] * noise_ref[:, cols].astype(F32)
        xn = xx[rows:, cols].astype(F32) + 0.5 * HEUN * (f0s[:, cols] + f) + kick
        xnb[:, cols] = xn.astype(BF16)
    resid = (obs_ref[...].astype(F32) - nn(xnb[...], c_ref[...])) * inv_ref[...]
    loglik = -0.5 * jnp.sum(resid * resid, axis=1, keepdims=True)

    peak = jnp.max(loglik, axis=0, keepdims=True)
    total = jnp.sum(jnp.exp(loglik - peak), axis=0, keepdims=True)
    norm_src[0] = jnp.where(iota((1, 128), 1) == 0, peak, total)
    exchange(2, norm_src, norm_tab, False)
    norm_tab[me] = norm_src[0]
    exchange_wait(2, norm_tab)
    table = norm_tab[...]
    peaks, totals = table[:, :, 0:1], table[:, :, 1:2]
    top = jnp.max(peaks, axis=0, keepdims=True)
    mass = jnp.sum(totals * jnp.exp(peaks - top), axis=0, keepdims=True)
    weight = jnp.exp(loglik - top[0]) / mass[0] * float(rows * devices)

    dmean = (weight * resid * inv_ref[...]).astype(BF16)
    for n in range(0, width, block):
        cols = slice(n, n + block)
        gxn = g_ref[:, cols].astype(F32) + nt(dmean, c_ref[cols, :])
        gxs[:, cols] = gxn
        gf[:rows, cols] = (0.5 * HEUN * gxn).astype(BF16)
    for n in range(0, hidden, block):
        cols = slice(n, n + block)
        one = nt(gf[:rows, :], w2_ref[cols, :]) * u1[:, cols]
        gp[:rows, cols] = one.astype(BF16)
        dots[:, cols] = jnp.sum(one, axis=0, keepdims=True)
    for n in range(0, width, block):
        cols = slice(n, n + block)
        gxn = gxs[:, cols]
        gxp = nt(gp[:rows, :], w1_ref[cols, :])
        both = gxn + gxp
        gf0 = 0.5 * HEUN * gxn + HEUN * gxp
        gf[rows:, cols] = gf0.astype(BF16)
        gxs[:, cols] = both
        d_b2 = jnp.sum(0.5 * HEUN * gxn + gf0, axis=0, keepdims=True)
        d_sigma = jnp.sum(both * noise_ref[:, cols].astype(F32), axis=0, keepdims=True)
        for j in range(block // 128):
            at = n // 128 + j
            accx[1, 1, at : at + 1, :] = d_b2[:, 128 * j : 128 * (j + 1)]
            accx[1, 2, at : at + 1, :] = d_sigma[:, 128 * j : 128 * (j + 1)]
    def core_swap(i, source, target):
        swap = pltpu.make_async_remote_copy(
            src_ref=source, dst_ref=target, send_sem=ssem.at[8 + i], recv_sem=rsem.at[12 + i],
            device_id=(other,), device_id_type=MESH,
        )
        swap.start()
        return swap

    theirs = pl.ds((1 - core) * chips, chips)
    accx[0] = tn(xnb[...], dmean).reshape(chips, 8, 128)
    for n in range(0, hidden, block):
        acc2[n // 8 : (n + block) // 8] = tn(aa[:, n : n + block], gf[...]).reshape(block // 8, 8, width)

    swaps = [core_swap(0, acc2.at[theirs], in2)]
    for n in range(0, hidden, block):
        cols = slice(n, n + block)
        zero = nt(gf[rows:, :], w2_ref[cols, :]) * u0[:, cols]
        gp[rows:, cols] = zero.astype(BF16)
        d_b1 = dots[:, cols] + jnp.sum(zero, axis=0, keepdims=True)
        for j in range(block // 128):
            at = n // 128 + j
            accx[1, 0, at : at + 1, :] = d_b1[:, 128 * j : 128 * (j + 1)]
    accx[1, 1, 4:8, :] = jnp.zeros((4, 128), F32)
    accx[1, 2, 4:8, :] = jnp.zeros((4, 128), F32)
    accx[1, pl.ds(3, chips - 3)] = jnp.zeros((chips - 3, 8, 128), F32)
    swaps.append(core_swap(1, accx.at[1 - core], inx))
    for h in range(2):
        acc1[h * chips : (h + 1) * chips] = tn(xx[...], gp[:, h * width : (h + 1) * width]).reshape(chips, 8, width)
    swaps.append(core_swap(2, acc1.at[theirs], in1))
    for n in range(0, width, block):
        cols = slice(n, n + block)
        gxs[:, cols] = gxs[:, cols] + nt(gp[rows:, :], w1_ref[cols, :])


    gx_high, gx_low = split(gxs[...])

    def give(i, carry):
        at = pl.multiple_of(i * group, group)
        onehot = jnp.where(iota((group * MOST, rows), 0) + at * MOST == flat, 1.0, 0.0).astype(BF16)
        out = nn(onehot, gx_high) + nn(onehot, gx_low)
        word, level = encode_wide(out.reshape(group, MOST, width))
        ret[pl.ds(at, group)] = jnp.concatenate([word, level], axis=1)
        return carry

    lax.fori_loop(0, devices // group, give, 0)
    for swap in swaps:
        swap.wait()

    step = 4

    def prepare(i, carry):
        at = pl.multiple_of(i * step, step)
        mine = pl.ds(at, step)
        held = pl.ds(core * chips + at, step)
        one = in1[mine] + acc1[held]
        two = in2[mine] + acc2[held]
        rest = inx[mine] + accx[core, mine]
        values = (one[:, :, :384], two[:, :, :384], joined([one[:, :, 384:], two[:, :, 384:], rest]))
        for t in range(3):
            sums[t, mine] = values[t]
            enc1[t, mine] = encode_slice(values[t])
        return carry

    lax.fori_loop(0, chips // step, prepare, 0)

    plane = chips // 4
    along = []
    for k in (2, 1, 3):
        for t, (axis, _, _) in enumerate(streams):
            there = lax.rem(coordinate[axis] + k, 4)
            copy = pltpu.make_async_remote_copy(
                src_ref=enc1.at[t, pl.ds(there * plane, plane)], dst_ref=got1.at[t, k - 1],
                send_sem=s1.at[3 * t + k - 1], recv_sem=r1.at[3 * t + k - 1],
                device_id=(me + (there - coordinate[axis]) * stride[axis],), device_id_type=MESH,
            )
            copy.start()
            along.append((t, copy))

    part_one = devices * 5 // 8
    exchange(3, ret, arr_ref, True, by_turn=True, high=part_one)
    arr_ref[0] = ret[me]

    home = [coordinate[axis] * plane for axis, _, _ in streams]
    spot = [coordinate[u] * 4 + coordinate[v] for _, u, v in streams]
    def over_plane(t, source, target, send_sem, recv_sem):
        axis, u, v = streams[t]
        base = core + coordinate[axis] * stride[axis]

        def send(k, carry):
            there = lax.rem(spot[t] + k, plane)
            d = base + lax.div(there, 4) * stride[u] + lax.rem(there, 4) * stride[v]
            pltpu.make_async_remote_copy(
                src_ref=source(there), dst_ref=target(k), send_sem=send_sem, recv_sem=recv_sem,
                device_id=(d,), device_id_type=MESH,
            ).start()
            return carry

        lax.fori_loop(1, plane, send, 0)

    for t in range(3):
        for stream, copy in along:
            if stream == t:
                copy.wait()

        def fold(i, carry):
            at = pl.multiple_of(i * step, step)
            value = sums[t, pl.ds(home[t] + at, step)]
            for k in range(3):
                value = value + joined(decode_slice(got1[t, k, pl.ds(at, step)]))
            half[t, pl.ds(at, step)] = value
            enc2[t, pl.ds(at, step)] = encode_slice(value)
            return carry

        lax.fori_loop(0, plane // step, fold, 0)
        over_plane(t, lambda there: enc2.at[t, there], lambda k: got2.at[t, k - 1], s2.at[t], r2.at[t])
    exchange(3, ret, arr_ref, True, by_turn=True, low=part_one)
    for t in range(3):
        bytes_wait(got2.at[t], r2.at[t])
        value = half[t, spot[t]][None]
        for k in range(0, plane - 1, 5):
            value = value + jnp.sum(joined(decode_slice(got2[t, k : k + 5])), axis=0, keepdims=True)
        fin[t] = encode_slice(value)
        whole[t, home[t] + spot[t]] = fin[t, 0]
        over_plane(t, lambda there: fin.at[t, 0], lambda k: whole.at[t, home[t] + spot[t]], s3.at[t], r3.at[t])

    outs = []

    def publish(i, t, first):
        source = whole.at[t, pl.ds(first, plane)]
        target = all_hbm.at[core, t, pl.ds(first, plane)]
        keep = pltpu.make_async_copy(source, target, out_sem.at[i])
        give = pltpu.make_async_remote_copy(
            src_ref=source, dst_ref=target, send_sem=s5.at[i], recv_sem=r5.at[i],
            device_id=(other,), device_id_type=MESH,
        )
        keep.start()
        give.start()
        outs.append(keep)
        outs.append(give)

    along = []
    for t, (axis, _, _) in enumerate(streams):
        bytes_wait(got2.at[t], r3.at[t])
        for k in (2, 1, 3):
            there = lax.rem(coordinate[axis] + k, 4)
            held = whole.at[t, pl.ds(home[t], plane)]
            copy = pltpu.make_async_remote_copy(
                src_ref=held, dst_ref=held, send_sem=s4.at[3 * t + k - 1], recv_sem=r4.at[3 * t + k - 1],
                device_id=(me + (there - coordinate[axis]) * stride[axis],), device_id_type=MESH,
            )
            copy.start()
            along.append((t, k, copy))
        publish(t, t, home[t])
    exchange_wait(3, arr_ref)

    def settle(i, carry):
        at = pl.multiple_of(i * group, group)
        column = wanted_columns(inc_ref[pl.ds(at, group)])
        onehot = jnp.where(column == iota((group, MOST, rows), 2).astype(F32), 1.0, 0.0)
        onehot = onehot.reshape(group * MOST, rows).astype(BF16)
        word = arr_ref[pl.ds(at, group)]
        value = decode_wide(word[:, :16], word[:, 16:17]).reshape(group * MOST, width)
        upper, lower = split(value)
        return carry + tn(onehot, upper) + tn(onehot, lower)

    dprev[...] = lax.fori_loop(0, devices // group, settle, jnp.zeros((rows, width), F32))
    settled = pltpu.make_async_copy(dprev, dprev_hbm, lsem.at[7])
    settled.start()

    for t, k, copy in along:
        copy.wait_recv()
        first = lax.rem(coordinate[streams[t][0]] + 4 - k, 4) * plane
        publish(3 + 3 * t + k - 1, t, first)
    for t, k, copy in along:
        copy.wait_send()
    for t in range(3):
        bytes_wait(got2.at[t], s2.at[t])
        bytes_wait(got2.at[t], s3.at[t])
    for copy in outs:
        copy.wait()
    settled.wait()


def finish_kernel(dp_ref, all_ref, dprev_ref, dw1_ref, dw2_ref, dc_ref, db1_ref, db2_ref, dsigma_ref):
    i = pl.program_id(0)
    step = all_ref.shape[2]
    width = dprev_ref.shape[1]
    dprev_ref[...] = dp_ref[...]
    for core in range(2):
        first, second, third = (decode_slice(all_ref[core, t]) for t in range(3))
        for b in range(4):
            one = first[b] if b < 3 else third[0]
            two = second[b] if b < 3 else third[1]
            at = core * width + 128 * b
            dw1_ref[:, at : at + 128] = one.reshape(step * 8, 128)
            dw2_ref[core, :, 128 * b : 128 * (b + 1)] = two.reshape(step * 8, 128)
        rest = third[2]
        if core == 0:
            dc_ref[...] = rest.reshape(step * 8, 128)
        else:

            @pl.when(i == 0)
            def _():
                db1_ref[...] = rest[0]
                db2_ref[...] = rest[1, :4]
                dsigma_ref[...] = rest[2, :4]


def per_device(x_prev, anc_owner, anc_row, noise, g_new, obs, w1, b1, w2, b2, c_obs, inv_scale, sigma):
    devices = lax.axis_size("particle")
    chips = devices // 2
    plane = chips // 4
    rows, width = x_prev.shape
    hidden = w1.shape[1]
    vmem = pl.BlockSpec(memory_space=pltpu.VMEM)
    anywhere = pl.BlockSpec(memory_space=pl.ANY)
    dma = pltpu.SemaphoreType.DMA
    d_prev, sums = pl.pallas_call(
        functools.partial(main_kernel, devices),
        out_shape=(
            jax.ShapeDtypeStruct((rows, width), F32),
            jax.ShapeDtypeStruct((2, 3, chips, 13, 128), I32),
        ),
        in_specs=[anywhere, vmem, vmem, anywhere, anywhere, anywhere, anywhere, vmem, anywhere, vmem, anywhere, vmem, vmem],
        out_specs=(anywhere, anywhere),
        scratch_shapes=[
            pltpu.VMEM((rows, width), BF16),
            pltpu.VMEM((rows, width), BF16),
            pltpu.VMEM((rows, width), BF16),
            pltpu.VMEM((rows, 128), BF16),
            pltpu.VMEM((width, hidden), BF16),
            pltpu.VMEM((hidden, width), BF16),
            pltpu.VMEM((width, 128), BF16),
            pltpu.VMEM((rows, width), F32),
            pltpu.VMEM((devices, 1, 128), F32),
            pltpu.VMEM((devices, 17, 128), I32),
            pltpu.VMEM((devices, 1, 128), F32),
            pltpu.VMEM((devices, 128), F32),
            pltpu.VMEM((devices, 2 * MOST, width // 2), BF16),
            pltpu.VMEM((devices, 2 * MOST, width // 2), BF16),
            pltpu.VMEM((1, 1, 128), F32),
            pltpu.VMEM((devices, 1, 128), F32),
            pltpu.VMEM((devices, 17, 128), I32),
            pltpu.VMEM((2 * rows, width), BF16),
            pltpu.VMEM((2 * rows, hidden), BF16),
            pltpu.VMEM((2 * rows, width), BF16),
            pltpu.VMEM((2 * rows, hidden), BF16),
            pltpu.VMEM((rows, hidden), F32),
            pltpu.VMEM((rows, hidden), F32),
            pltpu.VMEM((rows, width), BF16),
            pltpu.VMEM((rows, width), F32),
            pltpu.VMEM((rows, width), F32),
            pltpu.VMEM((1, hidden), F32),
            pltpu.VMEM((devices, 8, width), F32),
            pltpu.VMEM((devices, 8, width), F32),
            pltpu.VMEM((2, chips, 8, 128), F32),
            pltpu.VMEM((chips, 8, width), F32),
            pltpu.VMEM((chips, 8, width), F32),
            pltpu.VMEM((chips, 8, 128), F32),
            pltpu.VMEM((3, chips, 8, 384), F32),
            pltpu.VMEM((3, chips, 13, 128), I32),
            pltpu.VMEM((3, 3, plane, 13, 128), I32),
            pltpu.VMEM((3, plane, 8, 384), F32),
            pltpu.VMEM((3, plane, 13, 128), I32),
            pltpu.VMEM((3, plane - 1, 13, 128), I32),
            pltpu.VMEM((3, 1, 13, 128), I32),
            pltpu.VMEM((3, chips, 13, 128), I32),
            dma((12,)), dma((16,)), dma((8,)),
            dma((9,)), dma((9,)), dma((3,)), dma((3,)), dma((3,)), dma((3,)), dma((9,)), dma((9,)),
            dma((12,)), dma((12,)), dma((12,)),
        ],
        compiler_params=pltpu.CompilerParams(collective_id=0, has_side_effects=True, vmem_limit_bytes=58 * 2**20),
        name="heun_step",
    )(
        x_prev, anc_owner.reshape(1, rows), anc_row.reshape(1, rows), noise, g_new, obs,
        w1, b1.reshape(1, hidden), w2, b2.reshape(1, width), c_obs, inv_scale.reshape(1, -1), sigma.reshape(1, width),
    )
    step = 32
    lines = step * 8
    d_prev, d_w1, d_w2, d_c, d_b1, d_b2, d_sigma = pl.pallas_call(
        finish_kernel,
        grid=(chips // step,),
        out_shape=(
            jax.ShapeDtypeStruct((rows, width), F32),
            jax.ShapeDtypeStruct((width, hidden), F32),
            jax.ShapeDtypeStruct((2, hidden // 2, width), F32),
            jax.ShapeDtypeStruct((width, 128), F32),
            jax.ShapeDtypeStruct((hidden // 128, 128), F32),
            jax.ShapeDtypeStruct((width // 128, 128), F32),
            jax.ShapeDtypeStruct((width // 128, 128), F32),
        ),
        in_specs=[
            pl.BlockSpec((lines, width), lambda i: (i, 0)),
            pl.BlockSpec((2, 3, step, 13, 128), lambda i: (0, 0, i, 0, 0)),
        ],
        out_specs=(
            pl.BlockSpec((lines, width), lambda i: (i, 0)),
            pl.BlockSpec((lines, hidden), lambda i: (i, 0)),
            pl.BlockSpec((2, lines, width), lambda i: (0, i, 0)),
            pl.BlockSpec((lines, 128), lambda i: (i, 0)),
            pl.BlockSpec((hidden // 128, 128), lambda i: (0, 0)),
            pl.BlockSpec((width // 128, 128), lambda i: (0, 0)),
            pl.BlockSpec((width // 128, 128), lambda i: (0, 0)),
        ),
        compiler_params=pltpu.CompilerParams(vmem_limit_bytes=58 * 2**20),
        name="place_results",
    )(d_prev, sums)
    return (
        d_prev, d_w1, d_b1.reshape(hidden), d_w2.reshape(hidden, width), d_b2.reshape(width), d_c, d_sigma.reshape(width),
    )


def solution(mesh):
    split_rows = P("particle", None)
    return jax.shard_map(
        per_device,
        mesh=mesh,
        in_specs=(split_rows, split_rows, P("particle"), split_rows, split_rows, split_rows) + (P(),) * 7,
        out_specs=(split_rows, P(), P(), P(), P(), P(), P()),
        check_vma=False,
    )
```
